128 devices in a mesh: gx: 2 (over x_hi), gy: 4 (over y), gz: 16 (over x_lo, z, core).
Axes of the slice: x: 4 (x_hi: 2, x_lo: 2; x = x_hi * 2 + x_lo), y: 4, z: 4, core: 2. Of those that a mesh axis runs over, the one named last changes fastest.
Arguments:
- state_real: float32 [16777216], P(('gx', 'gy', 'gz'))
- state_imag: float32 [16777216], P(('gx', 'gy', 'gz'))
- adjoint_real: float32 [16777216], P(('gx', 'gy', 'gz'))
- adjoint_imag: float32 [16777216], P(('gx', 'gy', 'gz'))
- energies: int32 [16777216], P(('gx', 'gy', 'gz')), may hold values from 12 to 4324, as said below
- gamma_angle: float32 [1], replicated, may hold values from 0.02 to 0.1
- beta_angle: float32 [1], replicated, may hold values from 0.1 to 0.7
Outputs:
- input_real: float32 [16777216], P(('gx', 'gy', 'gz'))
- input_imag: float32 [16777216], P(('gx', 'gy', 'gz'))
- adjoint_in_real: float32 [16777216], P(('gx', 'gy', 'gz'))
- adjoint_in_imag: float32 [16777216], P(('gx', 'gy', 'gz'))
- gamma_gradient: float32 [1], replicated
- beta_gradient: float32 [1], replicated
The draws below stay inside these ranges and needn't reach their ends.
Inputs may be any that keep to these rules, and one draw needn't show every extreme that they name: `energies`: entry j is the LABS energy sum over k from 1 to 23 of (sum over i of s_i s_(i+k))^2, with spins s_i = 1 - 2 b_i from the bits b of j XOR a mask of 24 bits drawn once.
All inputs are finite; a program needn't handle non-finite values.
Results may differ from the reference program's by a relative error of at most 0.00013.
Values sent between devices are 32-bit elements; how exact they have to be, the bound alone decides.
A program may use at most 64 MiB of HBM per device.

```python
import math
import jax
import jax.numpy as jnp
from jax import lax

NQ = 24
STATE = 16777216


def count_ones_drawn(values, width):
    total = jnp.zeros_like(values)
    for bit_pos in range(width):
        total = total + (values >> bit_pos & 1)
    return total


def shared_parts(key):
    positions = jnp.arange(STATE, dtype=jnp.int32)
    subkeys = jax.random.split(key, 5)
    angles = jax.random.uniform(subkeys[0], (NQ,), jnp.float32, 0.6, 0.95)
    phases = jax.random.uniform(subkeys[1], (NQ,), jnp.float32, -0.8, 0.8)
    root_two = math.sqrt(2.0)
    prod_real = jnp.ones((STATE,), jnp.float32)
    prod_imag = jnp.zeros((STATE,), jnp.float32)
    for qubit_pos in range(NQ):
        chosen = (positions >> qubit_pos & 1).astype(jnp.float32)
        factor_real = root_two * (jnp.cos(angles[qubit_pos]) * (1.0 - chosen) + jnp.sin(angles[qubit_pos]) * jnp.cos(phases[qubit_pos]) * chosen)
        factor_imag = root_two * jnp.sin(angles[qubit_pos]) * jnp.sin(phases[qubit_pos]) * chosen
        prod_real, prod_imag = (prod_real * factor_real - prod_imag * factor_imag, prod_real * factor_imag + prod_imag * factor_real)
    noise_real = jax.random.normal(subkeys[2], (STATE,), jnp.float32)
    noise_imag = jax.random.normal(subkeys[3], (STATE,), jnp.float32)
    rising = jnp.exp(math.log(3.0) * positions.astype(jnp.float32) / STATE)
    weight = rising * jnp.exp(jax.random.uniform(subkeys[4], (STATE,), jnp.float32, 0.0, math.log(4.0)))
    return (prod_real + noise_real, prod_imag + noise_imag, weight)


def draw_state_real(key, part):
    state_part, other_part, weight = shared_parts(key)
    return state_part


def draw_state_imag(key, part):
    other_part, state_part, weight = shared_parts(key)
    return state_part


def draw_adjoint_real(key, part):
    state_part, other_part, weight = shared_parts(key)
    key = jax.random.fold_in(key, 5)
    noise = 0.7 * jax.random.normal(key, (STATE,), jnp.float32)
    return -weight * other_part / NQ + noise


def draw_adjoint_imag(key, part):
    state_part, other_part, weight = shared_parts(key)
    key = jax.random.fold_in(key, 7)
    noise = 0.7 * jax.random.normal(key, (STATE,), jnp.float32)
    return weight * state_part / NQ + noise


def draw_energies(key, part):
    key = jax.random.fold_in(key, 9)
    flip_mask = jax.random.randint(key, (), 0, 2 ** NQ, jnp.int32)
    positions = jnp.arange(STATE, dtype=jnp.int32) ^ flip_mask
    total = jnp.zeros((STATE,), jnp.int32)
    for lag_len in range(1, NQ):
        span_len = NQ - lag_len
        differ = count_ones_drawn((positions ^ positions >> lag_len) & (1 << span_len) - 1, span_len)
        correlation = span_len - 2 * differ
        total = total + correlation * correlation
    return total


def setup_inputs(seed: int = 0) -> dict:
    streams_of = jax.random.split(jax.random.key(seed), 8)
    return {
        "state_real": draw_state_real(jax.random.fold_in(streams_of[7], 71), 0),
        "state_imag": draw_state_imag(jax.random.fold_in(streams_of[7], 71), 0),
        "adjoint_real": draw_adjoint_real(jax.random.fold_in(streams_of[7], 71), 0),
        "adjoint_imag": draw_adjoint_imag(jax.random.fold_in(streams_of[7], 71), 0),
        "energies": draw_energies(jax.random.fold_in(streams_of[7], 71), 0),
        "gamma_angle": jnp.clip(jax.random.uniform(streams_of[5], (1,), jnp.float32, 0.02, 0.1), 0.02, 0.1),
        "beta_angle": jnp.clip(jax.random.uniform(streams_of[6], (1,), jnp.float32, 0.1, 0.7), 0.1, 0.7),
    }


def count_ones(values, width):
    total = jnp.zeros_like(values)
    for bit_pos in range(width):
        total = total + ((values >> bit_pos) & 1)
    return total


def hadamard(group_bits):
    indices = jnp.arange(2 ** group_bits, dtype=jnp.int32)
    parity = count_ones(indices[:, None] & indices[None, :], group_bits) & 1
    return (1 - 2 * parity).astype(jnp.float32) * jnp.float32(2.0 ** (-0.5 * group_bits))


def walsh_local(values, total_bits):
    finished = 0
    while finished < total_bits:
        group_bits = min(7, total_bits - finished)
        lower_size = 2 ** finished
        upper_size = values.shape[1] // (lower_size * 2 ** group_bits)
        matrix = hadamard(group_bits)
        if finished == 0:
            shaped = values.reshape(values.shape[0], upper_size, 2 ** group_bits)
            shaped = jnp.einsum("pak,km->pam", shaped, matrix, precision=lax.Precision.HIGHEST, preferred_element_type=jnp.float32)
        else:
            shaped = values.reshape(values.shape[0], upper_size, 2 ** group_bits, lower_size)
            shaped = jnp.einsum("pakl,km->paml", shaped, matrix, precision=lax.Precision.HIGHEST, preferred_element_type=jnp.float32)
        values = shaped.reshape(values.shape[0], -1)
        finished += group_bits
    return values


def rotate_pair(real_part, imag_part, cosine_part, sine_part):
    return real_part * cosine_part - imag_part * sine_part, real_part * sine_part + imag_part * cosine_part


def reference(state_real, state_imag, adjoint_real, adjoint_imag, energies, gamma_angle, beta_angle):
    stacked = jnp.stack([state_real, state_imag, adjoint_real, adjoint_imag])
    transformed = walsh_local(stacked, NQ)
    positions = jnp.arange(STATE, dtype=jnp.int32)
    eigenvalue = (NQ - 2 * count_ones(positions, NQ)).astype(jnp.float32)
    beta_total = jnp.sum(eigenvalue * (transformed[2] * transformed[1] - transformed[3] * transformed[0]))
    angle_beta = beta_angle[0] * eigenvalue
    cosine_part = jnp.cos(angle_beta)
    sine_part = jnp.sin(angle_beta)
    first_re, first_im = rotate_pair(transformed[0], transformed[1], cosine_part, sine_part)
    second_re, second_im = rotate_pair(transformed[2], transformed[3], cosine_part, sine_part)
    middle = walsh_local(jnp.stack([first_re, first_im, second_re, second_im]), NQ)
    energy_float = energies.astype(jnp.float32)
    gamma_total = jnp.sum(energy_float * (middle[2] * middle[1] - middle[3] * middle[0]))
    angle_gamma = gamma_angle[0] * energy_float
    cosine_cost = jnp.cos(angle_gamma)
    sine_cost = jnp.sin(angle_gamma)
    input_real, input_imag = rotate_pair(middle[0], middle[1], cosine_cost, sine_cost)
    adjoint_in_real, adjoint_in_imag = rotate_pair(middle[2], middle[3], cosine_cost, sine_cost)
    gamma_gradient = (gamma_total / STATE).reshape(1)
    beta_gradient = (beta_total / STATE).reshape(1)
    return input_real, input_imag, adjoint_in_real, adjoint_in_imag, gamma_gradient, beta_gradient
```

```python
import functools
import math

import jax
import jax.numpy as jnp
from jax import lax
from jax.experimental import pallas as pl
from jax.experimental.pallas import tpu as pltpu
from jax.sharding import PartitionSpec as P


MESH = pl.DeviceIdType.MESH
AXES = ("gx", "gy", "gz")
PARTS = (((0, 4), (4, 4), (8, 3)), ((11, 4), (15, 4), (19, 3)), ((22, 4), (26, 3), (29, 3)))
STEPS = 3


def sincos(angle):
    turns = jnp.floor(angle * jnp.float32(2.0 / math.pi) + 0.5)
    rest = angle - turns * jnp.float32(1.5703125)
    rest = rest - turns * jnp.float32(4.837512969970703125e-4)
    rest = rest - turns * jnp.float32(7.54978995489188216e-8)
    square = rest * rest
    sine = ((-1.9515295891e-4 * square + 8.3321608736e-3) * square - 1.6666654611e-1) * square * rest + rest
    cosine = (
        ((2.443315711809948e-5 * square - 1.388731625493765e-3) * square + 4.166664568298827e-2) * square * square
        - 0.5 * square
        + 1.0
    )
    quadrant = turns - 4.0 * jnp.floor(turns * 0.25)
    odd = (quadrant == 1.0) | (quadrant == 3.0)
    sine_out = jnp.where(odd, cosine, sine)
    cosine_out = jnp.where(odd, sine, cosine)
    sine_out = jnp.where(quadrant >= 2.0, -sine_out, sine_out)
    cosine_out = jnp.where((quadrant == 1.0) | (quadrant == 2.0), -cosine_out, cosine_out)
    return sine_out, cosine_out


def inner(a, s):
    return a[0] * s[1] - a[1] * s[0]


def add(u, v):
    return u[0] + v[0], u[1] + v[1]


def turn(c, s, own, other):
    return c * own[0] - s * other[1], c * own[1] + s * other[0]


def mix_four(cc, ss, sc, x):
    outer, middle = add(x[0], x[3]), add(x[1], x[2])
    outer_re, outer_im = sc * outer[0], sc * outer[1]
    middle_re, middle_im = sc * middle[0], sc * middle[1]
    y = []
    for own, far, near_re, near_im in (
        (x[0], x[3], middle_re, middle_im),
        (x[1], x[2], outer_re, outer_im),
        (x[2], x[1], outer_re, outer_im),
        (x[3], x[0], middle_re, middle_im),
    ):
        y.append((cc * own[0] - ss * far[0] - near_im, cc * own[1] - ss * far[1] + near_re))
    return y, outer, middle


def kernel(
    gamma_ref, beta_ref, sr, si, ar, ai, energy_hbm,
    o0, o1, o2, o3, gamma_out, beta_out,
    mid, home, other, home_b, local_in, energy, trig, outs, consts, lane_u, lane_a, total, relay, landed,
    t_send, t_recv, r_send, r_recv, c_send, c_recv, in_sem, out_sem, red_send, red_recv,
):
    gx, gy, gz = (lax.axis_index(name) for name in AXES)
    x_lo, z, core = gz // 8, (gz // 2) % 4, gz % 2
    flip_core = gz + 1 - 2 * core

    def flips(v):
        return v, v + 1 - 2 * (v % 2), v + 2 - 4 * (v // 2), 3 - v

    place = (2 * gx + x_lo, gy, z)
    blocks = tuple(flips(v) for v in place)
    x_flip = gz + 8 - 16 * x_lo
    peers = (
        (None, (gx, gy, x_flip), (1 - gx, gy, gz), (1 - gx, gy, x_flip)),
        (None,) + tuple((gx, blocks[1][k], gz) for k in (1, 2, 3)),
        (None,) + tuple((gx, gy, gz + 2 * (blocks[2][k] - z)) for k in (1, 2, 3)),
    )
    core_peer = (gx, gy, flip_core)
    group = []
    for k in range(4):
        base = gz + 2 * (blocks[2][k] - z)
        group += [(gx, gy, base), (gx, gy, base + 1 - 2 * core)]

    ins = (sr, si, ar, ai)

    loads = []
    for i, ref in enumerate(ins):
        loads.append(pltpu.make_async_copy(ref, local_in.at[i], in_sem.at[i]))
    loads.append(pltpu.make_async_copy(energy_hbm, energy, in_sem.at[4]))

    barrier = pltpu.get_barrier_semaphore()
    greeted = list(peers[0][1:]) + list(peers[1][1:]) + group[1:]
    for device in greeted:
        pl.semaphore_signal(barrier, inc=1, device_id=device, device_id_type=MESH)
    pl.semaphore_wait(barrier, len(greeted))

    def send(src, dst, send_sem, recv_sem, device):
        pltpu.make_async_remote_copy(
            src_ref=src, dst_ref=dst, send_sem=send_sem, recv_sem=recv_sem, device_id=device, device_id_type=MESH
        ).start()

    def wait_bytes(ref, sem):
        pltpu.make_async_copy(ref, ref, sem).wait()

    def start_there(f, p, j):
        axis = (p + f) % 3
        r0, n = PARTS[p][j]
        me, rows = place[axis], pl.ds(r0, n)
        ss, rs = t_send.at[f, 3 * p + j], t_recv.at[f, 3 * p + j]
        for k in (3, 1, 2):
            block = blocks[axis][k]
            if f == 0:
                for i, ref in enumerate(ins):
                    send(ref.at[block, rows], mid.at[f, me, i, rows], ss, rs, peers[axis][k])
            else:
                src = (home_b if f == 1 else home.at[1]).at[block, :, rows]
                send(src, mid.at[f, me, :, rows], ss, rs, peers[axis][k])
        if f == 0:
            for i, ref in enumerate(ins):
                pltpu.make_async_copy(ref.at[me, rows], mid.at[f, me, i, rows], rs).start()
        else:
            src = (home_b if f == 1 else home.at[1]).at[me, :, rows]
            pltpu.make_async_copy(src, mid.at[f, me, :, rows], rs).start()

    def start_back(f, p, j):
        axis = (p + f) % 3
        r0, n = PARTS[p][j]
        me, rows = place[axis], pl.ds(r0, n)
        ss, rs = r_send.at[f, 3 * p + j], r_recv.at[f, 3 * p + j]
        for k in (3, 1, 2):
            block = blocks[axis][k]
            send(mid.at[f, block, :, rows], home.at[f, me, :, rows], ss, rs, peers[axis][k])
        pltpu.make_async_copy(mid.at[f, me, :, rows], home.at[f, me, :, rows], rs).start()

    def wait_there(f, p, j):
        rows = pl.ds(*PARTS[p][j])
        wait_bytes(mid.at[f, :, :, rows], t_recv.at[f, 3 * p + j])

    def wait_back(f, p, j):
        rows = pl.ds(*PARTS[p][j])
        wait_bytes(home.at[f, :, :, rows], r_recv.at[f, 3 * p + j])

    def wait_sent(f, p, j):
        rows = pl.ds(*PARTS[p][j])
        wait_bytes(mid.at[f, pl.ds(0, 3), :, rows], t_send.at[f, 3 * p + j])
        wait_bytes(mid.at[f, pl.ds(0, 3), :, rows], r_send.at[f, 3 * p + j])

    zero = jnp.zeros((8, 128), jnp.float32)

    def mix_axis(f, p, j):
        r0, n = PARTS[p][j]
        cc, ss, sc = consts[0], consts[1], consts[2]

        def body(r, acc):
            x = [[(mid[f, b, 2 * v, r], mid[f, b, 2 * v + 1, r]) for b in range(4)] for v in range(2)]
            s, s_outer, s_middle = mix_four(cc, ss, sc, x[0])
            a, a_outer, a_middle = mix_four(cc, ss, sc, x[1])
            for v, y in ((0, s), (1, a)):
                for b in range(4):
                    mid[f, b, 2 * v, r] = y[b][0]
                    mid[f, b, 2 * v + 1, r] = y[b][1]
            return acc + inner(a_outer, s_middle) + inner(a_middle, s_outer)

        total[1] += lax.fori_loop(r0, r0 + n, body, zero)

    def mix_core_and_blocks(p, j):
        r0, n = PARTS[p][j]
        cc, ss, sc, c, sn = (consts[i] for i in range(5))

        def body(r, acc):
            x = []
            for v in range(2):
                x.append([])
                for b in range(4):
                    own = home[0, b, 2 * v, r], home[0, b, 2 * v + 1, r]
                    far = other[b, 2 * v, r], other[b, 2 * v + 1, r]
                    if v == 0:
                        x[v].append((own, far))
                    else:
                        acc = acc + inner(own, x[0][b][1])
                        x[v].append((own, far))
            x = [[turn(c, sn, own, far) for own, far in half] for half in x]
            s, s_outer, s_middle = mix_four(cc, ss, sc, x[0])
            a, a_outer, a_middle = mix_four(cc, ss, sc, x[1])
            for v, y in ((0, s), (1, a)):
                for b in range(4):
                    home_b[b, 2 * v, r] = y[b][0]
                    home_b[b, 2 * v + 1, r] = y[b][1]
            return acc + inner(a_outer, s_middle) + inner(a_middle, s_outer)

        total[1] += lax.fori_loop(r0, r0 + n, body, zero)

    sub = lax.broadcasted_iota(jnp.int32, (8, 128), 0)

    def far_row(x, bit):
        step = 1 << bit
        if bit == 2:
            return pltpu.roll(x, 4, 0)
        return jnp.where((sub >> bit) & 1 == 1, pltpu.roll(x, step, 0), pltpu.roll(x, 8 - step, 0))

    def mix_lanes(p, j):
        r0, n = PARTS[p][j]
        rows = pl.ds(r0, n)
        c, sn = consts[3], consts[4]
        acc = zero
        for b in range(4):
            pair = []
            for v in range(2):
                re = home[1, b, 2 * v, rows].reshape(n * 8, 128)
                im = home[1, b, 2 * v + 1, rows].reshape(n * 8, 128)
                pair.append(jnp.concatenate([re, im], axis=1))
            both = jnp.concatenate(pair, axis=0)
            near = jnp.dot(
                pair[0], lane_a[...], precision=lax.Precision.HIGHEST, preferred_element_type=jnp.float32
            )
            part = inner((pair[1][:, :128], pair[1][:, 128:]), (near[:, :128], near[:, 128:]))
            acc = acc + jnp.sum(part.reshape(n, 8, 128), axis=0)
            mixed = jnp.dot(
                both, lane_u[...], precision=lax.Precision.HIGHEST, preferred_element_type=jnp.float32
            )
            for v in range(2):
                home[1, b, 2 * v, rows] = mixed[v * n * 8 : (v + 1) * n * 8, :128].reshape(n, 8, 128)
                home[1, b, 2 * v + 1, rows] = mixed[v * n * 8 : (v + 1) * n * 8, 128:].reshape(n, 8, 128)

        def body(i, acc):
            b, r = i // n, r0 + i % n
            s = home[1, b, 0, r], home[1, b, 1, r]
            a = home[1, b, 2, r], home[1, b, 3, r]
            for bit in range(3):
                s_far = far_row(s[0], bit), far_row(s[1], bit)
                a_far = far_row(a[0], bit), far_row(a[1], bit)
                acc = acc + inner(a, s_far)
                s = turn(c, sn, s, s_far)
                a = turn(c, sn, a, a_far)
            home[1, b, 0, r] = s[0]
            home[1, b, 1, r] = s[1]
            home[1, b, 2, r] = a[0]
            home[1, b, 3, r] = a[1]
            return acc

        total[1] += lax.fori_loop(0, 4 * n, body, acc)

    for j in range(STEPS):
        for p in range(3):
            start_there(0, p, j)
    for load in loads:
        load.start()

    sn, c = sincos(jnp.full((8, 128), beta_ref[0], jnp.float32))
    consts[0] = c * c
    consts[1] = sn * sn
    consts[2] = sn * c
    consts[3] = c
    consts[4] = sn
    consts[5] = sn / c
    consts[6] = c * c * c * c * c
    total[0] = zero
    total[1] = zero

    def build_lanes():
        c_row, s_row = consts[3], consts[4]

        def body(i, carry):
            row = lax.broadcasted_iota(jnp.int32, (8, 128), 0) + 8 * i
            bits = row ^ lax.broadcasted_iota(jnp.int32, (8, 128), 1)
            size = jnp.ones((8, 128), jnp.float32)
            ones = jnp.zeros((8, 128), jnp.int32)
            for bit in range(7):
                on = (bits >> bit) & 1
                size = size * jnp.where(on == 1, s_row, c_row)
                ones = ones + on
            real = jnp.where(ones % 4 == 0, size, jnp.where(ones % 4 == 2, -size, 0.0))
            imag = jnp.where(ones % 4 == 1, size, jnp.where(ones % 4 == 3, -size, 0.0))
            near = jnp.where(ones == 1, 1.0, 0.0)
            upper = pl.ds(pl.multiple_of(8 * i, 8), 8)
            lower = pl.ds(pl.multiple_of(128 + 8 * i, 8), 8)
            lane_u[upper, :128] = real
            lane_u[upper, 128:] = imag
            lane_u[lower, :128] = -imag
            lane_u[lower, 128:] = real
            lane_a[upper, :128] = near
            lane_a[upper, 128:] = jnp.zeros((8, 128), jnp.float32)
            lane_a[lower, :128] = jnp.zeros((8, 128), jnp.float32)
            lane_a[lower, 128:] = near
            return carry

        lax.fori_loop(0, 16, body, 0)

    def build_trig():
        gamma = gamma_ref[0]

        def body(i, carry):
            b, r = i // 32, i % 32
            sine, cosine = sincos(gamma * energy[b, r].astype(jnp.float32))
            trig[0, b, r] = cosine * consts[6]
            trig[1, b, r] = sine * consts[6]
            return carry

        lax.fori_loop(0, 128, body, 0)

    def tile_bits_derivative():
        def body(i, acc):
            b, r = i // 32, i % 32
            near_re, near_im = zero, zero
            for bit in range(5):
                far = r + (1 << bit) - (2 << bit) * ((r // (1 << bit)) % 2)
                near_re = near_re + local_in[0, b, far]
                near_im = near_im + local_in[1, b, far]
            return acc + inner((local_in[2, b, r], local_in[3, b, r]), (near_re, near_im))

        total[1] += lax.fori_loop(0, 128, body, zero)

    build_lanes()
    for j in range(STEPS):
        for p in range(3):
            wait_there(0, p, j)
            mix_axis(0, p, j)
            start_back(0, p, j)
        if j == 0:
            for load in loads:
                load.wait()
            build_trig()
        if j == 1:
            tile_bits_derivative()

    for j in range(STEPS):
        for p in range(3):
            rows = pl.ds(*PARTS[p][j])
            wait_back(0, p, j)
            send(home.at[0, :, :, rows], other.at[:, :, rows], c_send.at[3 * p + j], c_recv.at[3 * p + j], core_peer)
        for p in range(3):
            rows = pl.ds(*PARTS[p][j])
            wait_bytes(other.at[:, :, rows], c_recv.at[3 * p + j])
            mix_core_and_blocks(p, j)
            start_there(1, p, j)
    for j in range(STEPS):
        for p in range(3):
            wait_there(1, p, j)
            mix_axis(1, p, j)
            start_back(1, p, j)
    for j in range(STEPS):
        for p in range(3):
            wait_back(1, p, j)
            mix_lanes(p, j)
            start_there(2, p, j)
    for j in range(STEPS):
        for p in range(3):
            wait_there(2, p, j)
            mix_axis(2, p, j)
            start_back(2, p, j)
    for j in range(STEPS):
        for p in range(3):
            rows = pl.ds(*PARTS[p][j])
            wait_sent(0, p, j)
            wait_sent(1, p, j)
            wait_bytes(other.at[:, :, rows], c_send.at[3 * p + j])
    for j in range(STEPS):
        for p in range(3):
            wait_back(2, p, j)

    t = consts[5]

    def tile_pair(u, v):
        return (
            (u[0] - t * v[1], u[1] + t * v[0]),
            (v[0] - t * u[1], v[1] + t * u[0]),
        )

    def low_bits(i, carry):
        b, first = i // 4, 8 * (i % 4)
        for v in range(2):
            x = [(home[2, b, 2 * v, first + k], home[2, b, 2 * v + 1, first + k]) for k in range(8)]
            for bit in range(3):
                for k in range(8):
                    if not k >> bit & 1:
                        x[k], x[k + (1 << bit)] = tile_pair(x[k], x[k + (1 << bit)])
            for k in range(8):
                home[2, b, 2 * v, first + k] = x[k][0]
                home[2, b, 2 * v + 1, first + k] = x[k][1]
        return carry

    def high_bits(b, i, acc):
        ys = []
        for v in range(2):
            x = [(home[2, b, 2 * v, 8 * k + i], home[2, b, 2 * v + 1, 8 * k + i]) for k in range(4)]
            x[0], x[1] = tile_pair(x[0], x[1])
            x[2], x[3] = tile_pair(x[2], x[3])
            x[0], x[2] = tile_pair(x[0], x[2])
            x[1], x[3] = tile_pair(x[1], x[3])
            ys.append(x)
        for k in range(4):
            r = 8 * k + i
            cosine, sine = trig[0, b, r], trig[1, b, r]
            s, a = ((y[k][0] * cosine - y[k][1] * sine, y[k][0] * sine + y[k][1] * cosine) for y in ys)
            outs[0, b, r] = s[0]
            outs[1, b, r] = s[1]
            outs[2, b, r] = a[0]
            outs[3, b, r] = a[1]
            acc = acc + energy[b, r].astype(jnp.float32) * inner(a, s)
        return acc

    lax.fori_loop(0, 16, low_bits, 0)
    acc = zero
    results = (o0, o1, o2, o3)
    for b in range(4):
        acc = lax.fori_loop(0, 8, functools.partial(high_bits, b), acc)
        for i in range(4):
            pltpu.make_async_copy(outs.at[i, b], results[i].at[b], out_sem.at[i, b]).start()
    total[0] = acc

    relay[0] = total[...]
    slot = 0
    for stage, (targets, first) in enumerate(((peers[0][1:], 0), (peers[1][1:], 3), (group[1:], 6))):
        count = len(targets)
        for k, device in enumerate(targets):
            send(relay.at[stage], landed.at[first + k], red_send.at[stage], red_recv.at[stage], device)
        if stage == 0:
            for j in range(STEPS):
                for p in range(3):
                    wait_sent(2, p, j)
        wait_bytes(landed.at[pl.ds(first, count)], red_recv.at[stage])
        terms = [relay[stage]] + [landed[first + k] for k in range(count)]
        while len(terms) > 1:
            terms = [terms[i] + terms[i + 1] for i in range(0, len(terms), 2)]
        relay[stage + 1] = terms[0]
    scale = jnp.float32(1.0 / 16777216.0)
    gamma_out[0] = jnp.sum(relay[3, 0]) * scale
    beta_out[0] = jnp.sum(relay[3, 1]) * scale
    for stage, count in ((0, 3), (1, 3), (2, 7)):
        wait_bytes(landed.at[pl.ds(0, count)], red_send.at[stage])
    for b in range(4):
        for i in range(4):
            pltpu.make_async_copy(outs.at[i, b], results[i].at[b], out_sem.at[i, b]).wait()


def per_device(state_real, state_imag, adjoint_real, adjoint_imag, energies, gamma_angle, beta_angle):
    shape = (4, 32, 8, 128)
    args = [v.reshape(shape) for v in (state_real, state_imag, adjoint_real, adjoint_imag, energies)]
    hbm = pl.BlockSpec(memory_space=pl.ANY)
    smem = pl.BlockSpec(memory_space=pltpu.SMEM)
    f32 = jnp.float32
    dma = pltpu.SemaphoreType.DMA
    big = jax.ShapeDtypeStruct(shape, f32)
    one = jax.ShapeDtypeStruct((1,), f32)
    results = pl.pallas_call(
        kernel,
        out_shape=(big, big, big, big, one, one),
        in_specs=[smem, smem] + [hbm] * 5,
        out_specs=(hbm, hbm, hbm, hbm, smem, smem),
        scratch_shapes=[
            pltpu.VMEM((3, 4, 4, 32, 8, 128), f32),
            pltpu.VMEM((3, 4, 4, 32, 8, 128), f32),
            pltpu.VMEM((4, 4, 32, 8, 128), f32),
            pltpu.VMEM((4, 4, 32, 8, 128), f32),
            pltpu.VMEM((4, 4, 32, 8, 128), f32),
            pltpu.VMEM(shape, jnp.int32),
            pltpu.VMEM((2,) + shape, f32),
            pltpu.VMEM((4,) + shape, f32),
            pltpu.VMEM((7, 8, 128), f32),
            pltpu.VMEM((256, 256), f32),
            pltpu.VMEM((256, 256), f32),
            pltpu.VMEM((2, 8, 128), f32),
            pltpu.VMEM((4, 2, 8, 128), f32),
            pltpu.VMEM((13, 2, 8, 128), f32),
            dma((3, 9)),
            dma((3, 9)),
            dma((3, 9)),
            dma((3, 9)),
            dma((9,)),
            dma((9,)),
            dma((5,)),
            dma((4, 4)),
            dma((3,)),
            dma((3,)),
        ],
        compiler_params=pltpu.CompilerParams(
            collective_id=0, has_side_effects=True, vmem_limit_bytes=50 << 20
        ),
        cost_estimate=pl.CostEstimate(flops=2 << 30, bytes_accessed=5 << 20, transcendentals=0),
    )(gamma_angle, beta_angle, *args)
    return tuple(v.reshape(-1) for v in results[:4]) + (results[4], results[5])


def solution(mesh):
    whole = P(AXES)
    return jax.shard_map(
        per_device,
        mesh=mesh,
        in_specs=(whole,) * 5 + (P(), P()),
        out_specs=(whole,) * 4 + (P(), P()),
        check_vma=False,
    )
```

```python
import functools
import math

import jax
import jax.numpy as jnp
from jax import lax
from jax.experimental import pallas as pl
from jax.experimental.pallas import tpu as pltpu
from jax.sharding import PartitionSpec as P


MESH = pl.DeviceIdType.MESH
AXES = ("gx", "gy", "gz")
STEPS = 3
EARLY = 1


def cut(first, count):
    sizes = [count // STEPS + (i < count % STEPS) for i in range(STEPS)]
    return tuple((first + sum(sizes[:i]), sizes[i]) for i in range(STEPS))


PARTS = (cut(0, 11), cut(11, 11), cut(22, 10))


def sincos(angle):
    turns = jnp.floor(angle * jnp.float32(2.0 / math.pi) + 0.5)
    rest = angle - turns * jnp.float32(1.5703125)
    rest = rest - turns * jnp.float32(4.837512969970703125e-4)
    rest = rest - turns * jnp.float32(7.54978995489188216e-8)
    square = rest * rest
    sine = ((-1.9515295891e-4 * square + 8.3321608736e-3) * square - 1.6666654611e-1) * square * rest + rest
    cosine = (
        ((2.443315711809948e-5 * square - 1.388731625493765e-3) * square + 4.166664568298827e-2) * square * square
        - 0.5 * square
        + 1.0
    )
    quadrant = turns - 4.0 * jnp.floor(turns * 0.25)
    odd = (quadrant == 1.0) | (quadrant == 3.0)
    sine_out = jnp.where(odd, cosine, sine)
    cosine_out = jnp.where(odd, sine, cosine)
    sine_out = jnp.where(quadrant >= 2.0, -sine_out, sine_out)
    cosine_out = jnp.where((quadrant == 1.0) | (quadrant == 2.0), -cosine_out, cosine_out)
    return sine_out, cosine_out


def inner(a, s):
    return a[0] * s[1] - a[1] * s[0]


def add(u, v):
    return u[0] + v[0], u[1] + v[1]


def turn(c, s, own, other):
    return c * own[0] - s * other[1], c * own[1] + s * other[0]


def mix_four(cc, ss, sc, x):
    outer, middle = add(x[0], x[3]), add(x[1], x[2])
    outer_re, outer_im = sc * outer[0], sc * outer[1]
    middle_re, middle_im = sc * middle[0], sc * middle[1]
    y = []
    for own, far, near_re, near_im in (
        (x[0], x[3], middle_re, middle_im),
        (x[1], x[2], outer_re, outer_im),
        (x[2], x[1], outer_re, outer_im),
        (x[3], x[0], middle_re, middle_im),
    ):
        y.append((cc * own[0] - ss * far[0] - near_im, cc * own[1] - ss * far[1] + near_re))
    return y, outer, middle


def kernel(
    gamma_ref, beta_ref, sr, si, ar, ai, energy_hbm,
    o0, o1, o2, o3, gamma_out, beta_out,
    mid, home, other, home_b, local_in, energy, energy_mid, trig, consts, lane_u, lane_a, total, relay, landed,
    t_send, t_recv, r_send, r_recv, c_send, c_recv, e_send, e_recv, in_sem, red_send, red_recv,
):
    gx, gy, gz = (lax.axis_index(name) for name in AXES)
    x_lo, z, core = gz // 8, (gz // 2) % 4, gz % 2
    flip_core = gz + 1 - 2 * core

    def flips(v):
        return v, v + 1 - 2 * (v % 2), v + 2 - 4 * (v // 2), 3 - v

    place = (2 * gx + x_lo, gy, z)
    blocks = tuple(flips(v) for v in place)
    x_flip = gz + 8 - 16 * x_lo
    peers = (
        (None, (gx, gy, x_flip), (1 - gx, gy, gz), (1 - gx, gy, x_flip)),
        (None,) + tuple((gx, blocks[1][k], gz) for k in (1, 2, 3)),
        (None,) + tuple((gx, gy, gz + 2 * (blocks[2][k] - z)) for k in (1, 2, 3)),
    )
    core_peer = (gx, gy, flip_core)
    group = []
    for k in range(4):
        base = gz + 2 * (blocks[2][k] - z)
        group += [(gx, gy, base), (gx, gy, base + 1 - 2 * core)]

    plane = []
    for i in range(4):
        over, along = ((gx, gz), (gx, x_flip), (1 - gx, gz), (1 - gx, x_flip))[i]
        plane += [(over, blocks[1][k], along) for k in range(4)]

    ins = (sr, si, ar, ai)

    loads = []
    for i, ref in enumerate(ins):
        loads.append(pltpu.make_async_copy(ref, local_in.at[:, i], in_sem.at[i]))
    loads.append(pltpu.make_async_copy(energy_hbm, energy, in_sem.at[4]))

    barrier = pltpu.get_barrier_semaphore()
    greeted = plane[1:] + group[1:]
    for device in greeted:
        pl.semaphore_signal(barrier, inc=1, device_id=device, device_id_type=MESH)
    for load in loads:
        load.start()

    def send(src, dst, send_sem, recv_sem, device):
        pltpu.make_async_remote_copy(
            src_ref=src, dst_ref=dst, send_sem=send_sem, recv_sem=recv_sem, device_id=device, device_id_type=MESH
        ).start()

    def wait_bytes(ref, sem):
        pltpu.make_async_copy(ref, ref, sem).wait()

    def start_there(f, p, j):
        axis = (p + f) % 3
        r0, n = PARTS[p][j]
        me, rows = place[axis], pl.ds(r0, n)
        ss, rs = t_send.at[f, STEPS * p + j], t_recv.at[f, STEPS * p + j]
        source = (local_in, home_b, home.at[1])[f]
        for k in (2, 3, 1):
            send(source.at[blocks[axis][k], :, rows], mid.at[f, me, :, rows], ss, rs, peers[axis][k])
        pltpu.make_async_copy(source.at[me, :, rows], mid.at[f, me, :, rows], rs).start()

    def part_rows(p):
        return pl.ds(PARTS[p][0][0], sum(n for _, n in PARTS[p]))

    def start_energy(p):
        axis, rows = (p + 2) % 3, part_rows(p)
        me = place[axis]
        for k in (2, 3, 1):
            block = blocks[axis][k]
            send(energy_hbm.at[block, rows], energy_mid.at[me, rows], e_send.at[p], e_recv.at[p], peers[axis][k])
        pltpu.make_async_copy(energy_hbm.at[me, rows], energy_mid.at[me, rows], e_recv.at[p]).start()

    def wait_energy(p):
        wait_bytes(energy_mid.at[:, part_rows(p)], e_recv.at[p])
        wait_bytes(energy_mid.at[pl.ds(0, 3), part_rows(p)], e_send.at[p])

    def start_back(f, p, j):
        axis = (p + f) % 3
        r0, n = PARTS[p][j]
        me, rows = place[axis], pl.ds(r0, n)
        ss, rs = r_send.at[f, STEPS * p + j], r_recv.at[f, STEPS * p + j]
        for k in (2, 3, 1):
            block = blocks[axis][k]
            send(mid.at[f, block, :, rows], home.at[f, me, :, rows], ss, rs, peers[axis][k])
        pltpu.make_async_copy(mid.at[f, me, :, rows], home.at[f, me, :, rows], rs).start()

    def wait_there(f, p, j):
        rows = pl.ds(*PARTS[p][j])
        wait_bytes(mid.at[f, :, :, rows], t_recv.at[f, STEPS * p + j])

    def wait_back(f, p, j):
        rows = pl.ds(*PARTS[p][j])
        wait_bytes(home.at[f, :, :, rows], r_recv.at[f, STEPS * p + j])

    def wait_sent(f, p, j):
        rows = pl.ds(*PARTS[p][j])
        wait_bytes(mid.at[f, pl.ds(0, 3), :, rows], t_send.at[f, STEPS * p + j])
        wait_bytes(mid.at[f, pl.ds(0, 3), :, rows], r_send.at[f, STEPS * p + j])

    zero = jnp.zeros((8, 128), jnp.float32)

    sub = lax.broadcasted_iota(jnp.int32, (8, 128), 0)

    def far_row(x, bit):
        step = 1 << bit
        if bit == 2:
            return pltpu.roll(x, 4, 0)
        return jnp.where((sub >> bit) & 1 == 1, pltpu.roll(x, step, 0), pltpu.roll(x, 8 - step, 0))

    def mix_axis(f, p, j):
        r0, n = PARTS[p][j]
        cc, ss, sc = (consts[i + (5 if f == 0 else 0)] for i in range(3))
        c, sn = consts[3], consts[4]

        def body(r, accs):
            acc, acc_gamma = accs
            x = [[(mid[f, b, 2 * v, r], mid[f, b, 2 * v + 1, r]) for b in range(4)] for v in range(2)]
            s, s_outer, s_middle = mix_four(cc, ss, sc, x[0])
            a, a_outer, a_middle = mix_four(cc, ss, sc, x[1])
            acc = acc + inner(a_outer, s_middle) + inner(a_middle, s_outer)
            for b in range(4):
                if f == 1:
                    for bit in range(3):
                        s_far = far_row(s[b][0], bit), far_row(s[b][1], bit)
                        a_far = far_row(a[b][0], bit), far_row(a[b][1], bit)
                        acc = acc + inner(a[b], s_far)
                        s[b] = turn(c, sn, s[b], s_far)
                        a[b] = turn(c, sn, a[b], a_far)
                if f == 2:
                    acc_gamma = acc_gamma + energy_mid[b, r].astype(jnp.float32) * inner(a[b], s[b])
                mid[f, b, 0, r] = s[b][0]
                mid[f, b, 1, r] = s[b][1]
                mid[f, b, 2, r] = a[b][0]
                mid[f, b, 3, r] = a[b][1]
            return acc, acc_gamma

        acc, acc_gamma = lax.fori_loop(r0, r0 + n, body, (zero, zero))
        total[1] += acc * consts[8] if f == 0 else acc
        if f == 2:
            total[0] += acc_gamma

    def mix_core_and_blocks(p, j):
        r0, n = PARTS[p][j]
        cc, ss, sc, c, sn = (consts[i] for i in range(5))

        def body(r, acc):
            x = []
            for v in range(2):
                x.append([])
                for b in range(4):
                    own = home[0, b, 2 * v, r], home[0, b, 2 * v + 1, r]
                    far = other[b, 2 * v, r], other[b, 2 * v + 1, r]
                    if v == 0:
                        x[v].append((own, far))
                    else:
                        acc = acc + inner(own, x[0][b][1])
                        x[v].append((own, far))
            x = [[turn(c, sn, own, far) for own, far in half] for half in x]
            s, s_outer, s_middle = mix_four(cc, ss, sc, x[0])
            a, a_outer, a_middle = mix_four(cc, ss, sc, x[1])
            for v, y in ((0, s), (1, a)):
                for b in range(4):
                    home_b[b, 2 * v, r] = y[b][0]
                    home_b[b, 2 * v + 1, r] = y[b][1]
            return acc + inner(a_outer, s_middle) + inner(a_middle, s_outer)

        total[1] += lax.fori_loop(r0, r0 + n, body, zero)

    def mix_lanes(p, j):
        r0, n = PARTS[p][j]
        rows, size = pl.ds(r0, n), n * 8

        def halves(v):
            parts = []
            for b in range(4):
                re = home[1, b, 2 * v, rows].reshape(size, 128)
                im = home[1, b, 2 * v + 1, rows].reshape(size, 128)
                parts.append(jnp.concatenate([re, im], axis=1))
            full = jnp.concatenate(parts, axis=0)
            high = full.astype(jnp.bfloat16)
            return full, high, (full - high.astype(jnp.float32)).astype(jnp.bfloat16)

        dot = functools.partial(jnp.dot, preferred_element_type=jnp.float32)
        u_high, u_low, near = lane_u[0], lane_u[1], lane_a[...]
        _, s_high, s_low = halves(0)
        full, a_high, a_low = halves(1)
        s_near = dot(s_high, near) + dot(s_low, near)
        part = inner((full[:, :128], full[:, 128:]), (s_near[:, :128], s_near[:, 128:]))
        total[1] += jnp.sum(part.reshape(4 * n, 8, 128), axis=0)
        for v, (high, low) in enumerate(((s_high, s_low), (a_high, a_low))):
            mixed = dot(high, u_high) + (dot(low, u_high) + dot(high, u_low))
            for b in range(4):
                home[1, b, 2 * v, rows] = mixed[b * size : (b + 1) * size, :128].reshape(n, 8, 128)
                home[1, b, 2 * v + 1, rows] = mixed[b * size : (b + 1) * size, 128:].reshape(n, 8, 128)

    sn, c = sincos(jnp.full((8, 128), beta_ref[0], jnp.float32))
    scale_tiles = c * c * c * c * c
    tangent = sn / c
    for i, value in enumerate((c * c, sn * sn, sn * c, c, sn)):
        consts[i] = value
    for i in range(3):
        consts[5 + i] = consts[i] * scale_tiles
    consts[8] = scale_tiles * scale_tiles
    total[0] = zero
    total[1] = zero

    def tile_pair(u, v):
        return (
            (u[0] - tangent * v[1], u[1] + tangent * v[0]),
            (v[0] - tangent * u[1], v[1] + tangent * u[0]),
        )

    def mix_tiles(b, v, places, bits):
        x = [(local_in[b, 2 * v, r], local_in[b, 2 * v + 1, r]) for r in places]
        for bit in range(bits):
            for k in range(1 << bits):
                if not k >> bit & 1:
                    x[k], x[k + (1 << bit)] = tile_pair(x[k], x[k + (1 << bit)])
        for r, (re, im) in zip(places, x):
            local_in[b, 2 * v, r] = re
            local_in[b, 2 * v + 1, r] = im

    def low_bits(i, carry):
        for v in range(2):
            mix_tiles(i // 4, v, [8 * (i % 4) + k for k in range(8)], 3)
        return carry

    def high_bits(i, carry):
        for v in range(2):
            mix_tiles(i // 8, v, [i % 8 + 8 * k for k in range(4)], 2)
        return carry

    pl.semaphore_wait(barrier, len(greeted))
    for p in range(3):
        start_energy(p)
    for load in loads[:4]:
        load.wait()
    lax.fori_loop(0, 16, low_bits, 0)
    lax.fori_loop(0, 32, high_bits, 0)

    for j in range(STEPS):
        for p in range(3):
            start_there(0, p, j)
    loads[4].wait()

    def build_lanes():
        c_row, s_row = (jnp.concatenate([consts[i], consts[i]], axis=0) for i in (3, 4))

        def body(i, carry):
            row = lax.broadcasted_iota(jnp.int32, (16, 128), 0) + 16 * i
            bits = row ^ lax.broadcasted_iota(jnp.int32, (16, 128), 1)
            size = jnp.ones((16, 128), jnp.float32)
            ones = jnp.zeros((16, 128), jnp.int32)
            for bit in range(7):
                on = (bits >> bit) & 1
                size = size * jnp.where(on == 1, s_row, c_row)
                ones = ones + on
            real = jnp.where(ones % 4 == 0, size, jnp.where(ones % 4 == 2, -size, 0.0))
            imag = jnp.where(ones % 4 == 1, size, jnp.where(ones % 4 == 3, -size, 0.0))
            near = jnp.where(ones == 1, 1.0, 0.0).astype(jnp.bfloat16)
            upper = pl.ds(pl.multiple_of(16 * i, 16), 16)
            lower = pl.ds(pl.multiple_of(128 + 16 * i, 16), 16)
            for rows, left, right in ((upper, real, imag), (lower, -imag, real)):
                for columns, value in ((slice(0, 128), left), (slice(128, 256), right)):
                    high = value.astype(jnp.bfloat16)
                    lane_u[0, rows, columns] = high
                    lane_u[1, rows, columns] = (value - high.astype(jnp.float32)).astype(jnp.bfloat16)
            lane_a[upper, :128] = near
            lane_a[upper, 128:] = jnp.zeros_like(near)
            lane_a[lower, :128] = jnp.zeros_like(near)
            lane_a[lower, 128:] = near
            return carry

        lax.fori_loop(0, 8, body, 0)

    def build_trig():
        gamma = gamma_ref[0]

        def body(i, carry):
            b, r = i // 32, i % 32
            sine, cosine = sincos(gamma * energy[b, r].astype(jnp.float32))
            trig[0, b, r] = cosine
            trig[1, b, r] = sine
            return carry

        lax.fori_loop(0, 128, body, 0)

    def tile_bits_derivative():
        def body(i, acc):
            b, r = i // 32, i % 32
            near_re, near_im = zero, zero
            for bit in range(5):
                far = r + (1 << bit) - (2 << bit) * ((r // (1 << bit)) % 2)
                near_re = near_re + local_in[b, 0, far]
                near_im = near_im + local_in[b, 1, far]
            return acc + inner((local_in[b, 2, r], local_in[b, 3, r]), (near_re, near_im))

        total[1] += lax.fori_loop(0, 128, body, zero) * consts[8]

    build_lanes()
    build_trig()
    tile_bits_derivative()
    for j in range(STEPS):
        for p in range(3):
            wait_there(0, p, j)
            mix_axis(0, p, j)
            start_back(0, p, j)

    for j in range(STEPS):
        for p in range(3):
            rows = pl.ds(*PARTS[p][j])
            wait_back(0, p, j)
            send(home.at[0, :, :, rows], other.at[:, :, rows], c_send.at[STEPS * p + j], c_recv.at[STEPS * p + j], core_peer)
        for p in range(3):
            rows = pl.ds(*PARTS[p][j])
            wait_bytes(other.at[:, :, rows], c_recv.at[STEPS * p + j])
            mix_core_and_blocks(p, j)
            start_there(1, p, j)
    for j in range(STEPS):
        for p in range(3):
            wait_there(1, p, j)
            mix_axis(1, p, j)
            start_back(1, p, j)
    for j in range(STEPS):
        for p in range(3):
            wait_back(1, p, j)
            mix_lanes(p, j)
            start_there(2, p, j)
    for p in range(3):
        wait_energy(p)
    for j in range(STEPS):
        for p in range(3):
            wait_there(2, p, j)
            mix_axis(2, p, j)
            if j < EARLY:
                start_back(2, p, j)

    stages = ((group[1:], 0), (plane[1:], 7))
    results = (o0, o1, o2, o3)

    def start_sum(stage):
        targets, first = stages[stage]
        for k, device in enumerate(targets):
            send(relay.at[stage, :2], landed.at[first + k, :2], red_send.at[stage], red_recv.at[stage], device)

    def finish_sum(stage):
        targets, first = stages[stage]
        count = len(targets)
        wait_bytes(landed.at[pl.ds(first, count), :2], red_recv.at[stage])
        terms = [relay[stage, :2]] + [landed[first + k, :2] for k in range(count)]
        while len(terms) > 1:
            terms = [terms[i] + terms[i + 1] for i in range(0, len(terms), 2)]
        relay[stage + 1, :2] = terms[0]

    def turn_back(p, j):
        r0, n = PARTS[p][j]

        def body(r, carry):
            for b in range(4):
                cosine, sine = trig[0, b, r], trig[1, b, r]
                for v in range(2):
                    re, im = home[2, b, 2 * v, r], home[2, b, 2 * v + 1, r]
                    results[2 * v][b, r] = re * cosine - im * sine
                    results[2 * v + 1][b, r] = re * sine + im * cosine
            return carry

        lax.fori_loop(r0, r0 + n, body, 0)

    for i in range(2):
        relay[0, i : i + 1] = jnp.sum(total[i], axis=0, keepdims=True)
    start_sum(0)
    for j in range(EARLY, STEPS):
        for p in range(3):
            start_back(2, p, j)
    for j in range(STEPS):
        for p in range(3):
            rows = pl.ds(*PARTS[p][j])
            wait_sent(0, p, j)
            wait_sent(1, p, j)
            wait_bytes(other.at[:, :, rows], c_send.at[STEPS * p + j])
    for j in range(STEPS):
        for p in range(3):
            wait_back(2, p, j)
            turn_back(p, j)
        if j == 0:
            finish_sum(0)
            start_sum(1)
    for j in range(STEPS):
        for p in range(3):
            wait_sent(2, p, j)
    finish_sum(1)
    scale = jnp.float32(1.0 / 16777216.0)
    gamma_out[0] = jnp.sum(relay[2, 0:1]) * scale
    beta_out[0] = jnp.sum(relay[2, 1:2]) * scale
    for stage, count in ((0, 7), (1, 15)):
        wait_bytes(landed.at[pl.ds(0, count), :2], red_send.at[stage])


def store_kernel(i0, i1, i2, i3, o0, o1, o2, o3, sem):
    copies = [pltpu.make_async_copy(i, o, sem.at[k]) for k, (i, o) in enumerate(((i0, o0), (i1, o1), (i2, o2), (i3, o3)))]
    for copy in copies:
        copy.start()
    for copy in copies:
        copy.wait()


def per_device(state_real, state_imag, adjoint_real, adjoint_imag, energies, gamma_angle, beta_angle):
    shape = (4, 32, 8, 128)
    args = [v.reshape(shape) for v in (state_real, state_imag, adjoint_real, adjoint_imag, energies)]
    hbm = pl.BlockSpec(memory_space=pltpu.HBM)
    vmem = pl.BlockSpec(memory_space=pltpu.VMEM)
    smem = pl.BlockSpec(memory_space=pltpu.SMEM)
    f32 = jnp.float32
    dma = pltpu.SemaphoreType.DMA
    big = pltpu.VMEM(shape, f32)
    one = jax.ShapeDtypeStruct((1,), f32)
    results = pl.pallas_call(
        kernel,
        out_shape=(big, big, big, big, one, one),
        in_specs=[smem, smem] + [hbm] * 5,
        out_specs=(vmem, vmem, vmem, vmem, smem, smem),
        scratch_shapes=[
            pltpu.VMEM((3, 4, 4, 32, 8, 128), f32),
            pltpu.VMEM((3, 4, 4, 32, 8, 128), f32),
            pltpu.VMEM((4, 4, 32, 8, 128), f32),
            pltpu.VMEM((4, 4, 32, 8, 128), f32),
            pltpu.VMEM((4, 4, 32, 8, 128), f32),
            pltpu.VMEM(shape, jnp.int32),
            pltpu.VMEM(shape, jnp.int32),
            pltpu.VMEM((2,) + shape, f32),
            pltpu.VMEM((9, 8, 128), f32),
            pltpu.VMEM((2, 256, 256), jnp.bfloat16),
            pltpu.VMEM((256, 256), jnp.bfloat16),
            pltpu.VMEM((2, 8, 128), f32),
            pltpu.VMEM((3, 8, 128), f32),
            pltpu.VMEM((22, 8, 128), f32),
            dma((3, 3 * STEPS)),
            dma((3, 3 * STEPS)),
            dma((3, 3 * STEPS)),
            dma((3, 3 * STEPS)),
            dma((3 * STEPS,)),
            dma((3 * STEPS,)),
            dma((3,)),
            dma((3,)),
            dma((5,)),
            dma((2,)),
            dma((2,)),
        ],
        compiler_params=pltpu.CompilerParams(
            collective_id=0, has_side_effects=True, vmem_limit_bytes=58 << 20
        ),
        cost_estimate=pl.CostEstimate(flops=2 << 30, bytes_accessed=5 << 20, transcendentals=0),
    )(gamma_angle, beta_angle, *args)
    moved = pl.pallas_call(
        store_kernel,
        out_shape=(jax.ShapeDtypeStruct(shape, f32),) * 4,
        in_specs=[vmem] * 4,
        out_specs=(pl.BlockSpec(memory_space=pltpu.HBM),) * 4,
        scratch_shapes=[dma((4,))],
    )(*(pltpu.with_memory_space_constraint(v, pltpu.VMEM) for v in results[:4]))
    return tuple(v.reshape(-1) for v in moved) + (results[4], results[5])


def solution(mesh):
    whole = P(AXES)
    return jax.shard_map(
        per_device,
        mesh=mesh,
        in_specs=(whole,) * 5 + (P(), P()),
        out_specs=(whole,) * 4 + (P(), P()),
        check_vma=False,
    )
```

```python
import functools
import math

import jax
import jax.numpy as jnp
from jax import lax
from jax.experimental import pallas as pl
from jax.experimental.pallas import tpu as pltpu
from jax.sharding import PartitionSpec as P


MESH = pl.DeviceIdType.MESH
AXES = ("gx", "gy", "gz")
STEPS = 4
EARLY = 2


def core_first(p, j):
    return j % 2 == 1


STORES = 4


def cut(first, count):
    sizes = [count // STEPS + (STEPS - 1 - i < count % STEPS) for i in range(STEPS)]
    return tuple((first + sum(sizes[:i]), sizes[i]) for i in range(STEPS))


PARTS = (cut(0, 11), cut(11, 11), cut(22, 10))


def sincos(angle):
    turns = jnp.floor(angle * jnp.float32(2.0 / math.pi) + 0.5)
    rest = angle - turns * jnp.float32(1.5703125)
    rest = rest - turns * jnp.float32(4.837512969970703125e-4)
    rest = rest - turns * jnp.float32(7.54978995489188216e-8)
    square = rest * rest
    sine = ((-1.9515295891e-4 * square + 8.3321608736e-3) * square - 1.6666654611e-1) * square * rest + rest
    cosine = (
        ((2.443315711809948e-5 * square - 1.388731625493765e-3) * square + 4.166664568298827e-2) * square * square
        - 0.5 * square
        + 1.0
    )
    quadrant = turns - 4.0 * jnp.floor(turns * 0.25)
    odd = (quadrant == 1.0) | (quadrant == 3.0)
    sine_out = jnp.where(odd, cosine, sine)
    cosine_out = jnp.where(odd, sine, cosine)
    sine_out = jnp.where(quadrant >= 2.0, -sine_out, sine_out)
    cosine_out = jnp.where((quadrant == 1.0) | (quadrant == 2.0), -cosine_out, cosine_out)
    return sine_out, cosine_out


def inner(a, s):
    return a[0] * s[1] - a[1] * s[0]


def add(u, v):
    return u[0] + v[0], u[1] + v[1]


def turn(c, s, own, other):
    return c * own[0] - s * other[1], c * own[1] + s * other[0]


def mix_four(cc, ss, sc, x):
    outer, middle = add(x[0], x[3]), add(x[1], x[2])
    outer_re, outer_im = sc * outer[0], sc * outer[1]
    middle_re, middle_im = sc * middle[0], sc * middle[1]
    y = []
    for own, far, near_re, near_im in (
        (x[0], x[3], middle_re, middle_im),
        (x[1], x[2], outer_re, outer_im),
        (x[2], x[1], outer_re, outer_im),
        (x[3], x[0], middle_re, middle_im),
    ):
        y.append((cc * own[0] - ss * far[0] - near_im, cc * own[1] - ss * far[1] + near_re))
    return y, outer, middle


def kernel(
    gamma_ref, beta_ref, sr, si, ar, ai, energy_hbm,
    o0, o1, o2, o3, gamma_out, beta_out,
    mid, home, other, home_b, local_in, energy, energy_mid, trig, consts, lane_u, lane_a, total, relay, landed,
    t_send, t_recv, r_send, r_recv, c_send, c_recv, e_send, e_recv, in_sem, red_send, red_recv,
):
    gx, gy, gz = (lax.axis_index(name) for name in AXES)
    x_lo, z, core = gz // 8, (gz // 2) % 4, gz % 2
    flip_core = gz + 1 - 2 * core

    def flips(v):
        return v, v + 1 - 2 * (v % 2), v + 2 - 4 * (v // 2), 3 - v

    place = (2 * gx + x_lo, gy, z)
    blocks = tuple(flips(v) for v in place)
    x_flip = gz + 8 - 16 * x_lo
    peers = (
        (None, (gx, gy, x_flip), (1 - gx, gy, gz), (1 - gx, gy, x_flip)),
        (None,) + tuple((gx, blocks[1][k], gz) for k in (1, 2, 3)),
        (None,) + tuple((gx, gy, gz + 2 * (blocks[2][k] - z)) for k in (1, 2, 3)),
    )
    core_peer = (gx, gy, flip_core)
    group = []
    for k in range(4):
        base = gz + 2 * (blocks[2][k] - z)
        group += [(gx, gy, base), (gx, gy, base + 1 - 2 * core)]

    plane = []
    for i in range(4):
        over, along = ((gx, gz), (gx, x_flip), (1 - gx, gz), (1 - gx, x_flip))[i]
        plane += [(over, blocks[1][k], along) for k in range(4)]

    ins = (sr, si, ar, ai)

    loads = []
    for i, ref in enumerate(ins):
        loads.append(pltpu.make_async_copy(ref, local_in.at[:, i], in_sem.at[i]))
    loads.append(pltpu.make_async_copy(energy_hbm, energy, in_sem.at[4]))

    barrier = pltpu.get_barrier_semaphore()
    greeted = [core_peer] + [peers[axis][k] for axis in range(3) for k in (1, 2, 3)]
    for load in loads:
        load.start()
    for device in greeted:
        pl.semaphore_signal(barrier, inc=1, device_id=device, device_id_type=MESH)

    def send(src, dst, send_sem, recv_sem, device):
        pltpu.make_async_remote_copy(
            src_ref=src, dst_ref=dst, send_sem=send_sem, recv_sem=recv_sem, device_id=device, device_id_type=MESH
        ).start()

    def wait_bytes(ref, sem):
        pltpu.make_async_copy(ref, ref, sem).wait()

    def source_of(f, p, j):
        if f == 0:
            return local_in
        return home_b if core_first(p, j) == (f == 1) else home.at[f - 1]

    def start_there(f, p, j, arrays=slice(None)):
        axis = (p + f) % 3
        r0, n = PARTS[p][j]
        rows = pl.ds(r0, n)
        ss, rs = t_send.at[f, STEPS * p + j], t_recv.at[f, STEPS * p + j]
        source = source_of(f, p, j)
        for k in (2, 3, 1):
            send(source.at[blocks[axis][k], arrays, rows], mid.at[f, k - 1, arrays, rows], ss, rs, peers[axis][k])

    def part_rows(p):
        return pl.ds(PARTS[p][0][0], sum(n for _, n in PARTS[p]))

    def start_energy(p):
        axis, rows = (p + 2) % 3, part_rows(p)
        for k in (2, 3, 1):
            block = blocks[axis][k]
            send(energy_hbm.at[block, rows], energy_mid.at[k - 1, rows], e_send.at[p], e_recv.at[p], peers[axis][k])

    def wait_energy(p):
        wait_bytes(energy_mid.at[:, part_rows(p)], e_recv.at[p])
        wait_bytes(energy_mid.at[:, part_rows(p)], e_send.at[p])

    def start_back(f, p, j):
        axis = (p + f) % 3
        r0, n = PARTS[p][j]
        me, rows = place[axis], pl.ds(r0, n)
        ss, rs = r_send.at[f, STEPS * p + j], r_recv.at[f, STEPS * p + j]
        for k in (2, 3, 1):
            send(mid.at[f, k - 1, :, rows], home.at[f, me, :, rows], ss, rs, peers[axis][k])

    def wait_there(f, p, j):
        rows = pl.ds(*PARTS[p][j])
        wait_bytes(mid.at[f, :, :, rows], t_recv.at[f, STEPS * p + j])

    def wait_back(f, p, j):
        rows = pl.ds(*PARTS[p][j])
        wait_bytes(mid.at[f, :, :, rows], r_recv.at[f, STEPS * p + j])

    def wait_sent(f, p, j):
        rows = pl.ds(*PARTS[p][j])
        wait_bytes(mid.at[f, :, :, rows], t_send.at[f, STEPS * p + j])
        wait_bytes(mid.at[f, :, :, rows], r_send.at[f, STEPS * p + j])

    zero = jnp.zeros((8, 128), jnp.float32)

    sub = lax.broadcasted_iota(jnp.int32, (8, 128), 0)

    def far_row(x, bit):
        step = 1 << bit
        if bit == 2:
            return pltpu.roll(x, 4, 0)
        return jnp.where((sub >> bit) & 1 == 1, pltpu.roll(x, step, 0), pltpu.roll(x, 8 - step, 0))

    def mix_axis(f, p, j):
        r0, n = PARTS[p][j]
        me, source = place[(p + f) % 3], source_of(f, p, j)
        cc, ss, sc = (consts[i + (5 if f == 0 else 0)] for i in range(3))
        c, sn = consts[3], consts[4]

        def body(r, accs):
            acc, acc_gamma = accs
            x = []
            for v in range(2):
                own = source[me, 2 * v, r], source[me, 2 * v + 1, r]
                x.append([own] + [(mid[f, k, 2 * v, r], mid[f, k, 2 * v + 1, r]) for k in range(3)])
            s, s_outer, s_middle = mix_four(cc, ss, sc, x[0])
            a, a_outer, a_middle = mix_four(cc, ss, sc, x[1])
            acc = acc + inner(a_outer, s_middle) + inner(a_middle, s_outer)
            for b in range(4):
                if f == 1:
                    for bit in range(3):
                        s_far = far_row(s[b][0], bit), far_row(s[b][1], bit)
                        a_far = far_row(a[b][0], bit), far_row(a[b][1], bit)
                        acc = acc + inner(a[b], s_far)
                        s[b] = turn(c, sn, s[b], s_far)
                        a[b] = turn(c, sn, a[b], a_far)
                if f == 2:
                    level = energy_mid[b - 1, r] if b else energy[me, r]
                    acc_gamma = acc_gamma + level.astype(jnp.float32) * inner(a[b], s[b])
                for i, value in enumerate((*s[b], *a[b])):
                    if b:
                        mid[f, b - 1, i, r] = value
                    else:
                        home[f, me, i, r] = value
            return acc, acc_gamma

        acc, acc_gamma = lax.fori_loop(r0, r0 + n, body, (zero, zero))
        total[1] += acc * consts[8] if f == 0 else acc
        if f == 2:
            total[0] += acc_gamma

    def mix_core_and_blocks(f, p, j):
        r0, n = PARTS[p][j]
        cc, ss, sc, c, sn = (consts[i] for i in range(5))

        def body(r, acc):
            x = []
            for v in range(2):
                x.append([])
                for b in range(4):
                    own = home[f, b, 2 * v, r], home[f, b, 2 * v + 1, r]
                    far = other[b, 2 * v, r], other[b, 2 * v + 1, r]
                    if v == 0:
                        x[v].append((own, far))
                    else:
                        acc = acc + inner(own, x[0][b][1])
                        x[v].append((own, far))
            x = [[turn(c, sn, own, far) for own, far in half] for half in x]
            s, s_outer, s_middle = mix_four(cc, ss, sc, x[0])
            a, a_outer, a_middle = mix_four(cc, ss, sc, x[1])
            for v, y in ((0, s), (1, a)):
                for b in range(4):
                    home_b[b, 2 * v, r] = y[b][0]
                    home_b[b, 2 * v + 1, r] = y[b][1]
            return acc + inner(a_outer, s_middle) + inner(a_middle, s_outer)

        total[1] += lax.fori_loop(r0, r0 + n, body, zero)

    def mix_lanes(f, p, j):
        r0, n = PARTS[p][j]
        rows, size = pl.ds(r0, n), n * 8

        def halves(v):
            parts = []
            for b in range(4):
                re = home[f, b, 2 * v, rows].reshape(size, 128)
                im = home[f, b, 2 * v + 1, rows].reshape(size, 128)
                parts.append(jnp.concatenate([re, im], axis=1))
            full = jnp.concatenate(parts, axis=0)
            high = full.astype(jnp.bfloat16)
            return full, high, (full - high.astype(jnp.float32)).astype(jnp.bfloat16)

        dot = functools.partial(jnp.dot, preferred_element_type=jnp.float32)
        u_high, u_low, near = lane_u[0], lane_u[1], lane_a[...]
        _, s_high, s_low = halves(0)
        full, a_high, a_low = halves(1)
        s_near = dot(s_high, near) + dot(s_low, near)
        part = inner((full[:, :128], full[:, 128:]), (s_near[:, :128], s_near[:, 128:]))
        total[1] += jnp.sum(part.reshape(4 * n, 8, 128), axis=0)
        for v, (high, low) in enumerate(((s_high, s_low), (a_high, a_low))):
            mixed = dot(high, u_high) + (dot(low, u_high) + dot(high, u_low))
            for b in range(4):
                home[f, b, 2 * v, rows] = mixed[b * size : (b + 1) * size, :128].reshape(n, 8, 128)
                home[f, b, 2 * v + 1, rows] = mixed[b * size : (b + 1) * size, 128:].reshape(n, 8, 128)

    sn, c = sincos(jnp.full((8, 128), beta_ref[0], jnp.float32))
    scale_tiles = c * c * c * c * c
    tangent = sn / c
    for i, value in enumerate((c * c, sn * sn, sn * c, c, sn)):
        consts[i] = value
    for i in range(3):
        consts[5 + i] = consts[i] * scale_tiles
    consts[8] = scale_tiles * scale_tiles
    total[0] = zero
    total[1] = zero

    def tile_pair(u, v):
        return (
            (u[0] - tangent * v[1], u[1] + tangent * v[0]),
            (v[0] - tangent * u[1], v[1] + tangent * u[0]),
        )

    def mix_tiles(b, v, places, bits):
        x = [(local_in[b, 2 * v, r], local_in[b, 2 * v + 1, r]) for r in places]
        for bit in range(bits):
            for k in range(1 << bits):
                if not k >> bit & 1:
                    x[k], x[k + (1 << bit)] = tile_pair(x[k], x[k + (1 << bit)])
        for r, (re, im) in zip(places, x):
            local_in[b, 2 * v, r] = re
            local_in[b, 2 * v + 1, r] = im

    def low_bits(v, i, carry):
        mix_tiles(i // 4, v, [8 * (i % 4) + k for k in range(8)], 3)
        return carry

    def high_bits(v, i, carry):
        for half in range(2):
            mix_tiles(i // 4, v, [2 * (i % 4) + half + 8 * k for k in range(4)], 2)
        return carry

    pl.semaphore_wait(barrier, len(greeted))
    for p in range(3):
        start_energy(p)
    for v in range(2):
        for load in loads[2 * v : 2 * v + 2]:
            load.wait()
        lax.fori_loop(0, 16, functools.partial(low_bits, v), 0)
        lax.fori_loop(0, 16, functools.partial(high_bits, v), 0)
        for p in range(3):
            start_there(0, p, 0, pl.ds(2 * v, 2))
    for j in range(1, STEPS):
        for p in range(3):
            start_there(0, p, j)
    loads[4].wait()

    def build_lanes():
        c_row, s_row = (jnp.concatenate([consts[i], consts[i]], axis=0) for i in (3, 4))

        def body(i, carry):
            row = lax.broadcasted_iota(jnp.int32, (16, 128), 0) + 16 * i
            bits = row ^ lax.broadcasted_iota(jnp.int32, (16, 128), 1)
            size = jnp.ones((16, 128), jnp.float32)
            ones = jnp.zeros((16, 128), jnp.int32)
            for bit in range(7):
                on = (bits >> bit) & 1
                size = size * jnp.where(on == 1, s_row, c_row)
                ones = ones + on
            real = jnp.where(ones % 4 == 0, size, jnp.where(ones % 4 == 2, -size, 0.0))
            imag = jnp.where(ones % 4 == 1, size, jnp.where(ones % 4 == 3, -size, 0.0))
            near = jnp.where(ones == 1, 1.0, 0.0).astype(jnp.bfloat16)
            upper = pl.ds(pl.multiple_of(16 * i, 16), 16)
            lower = pl.ds(pl.multiple_of(128 + 16 * i, 16), 16)
            for rows, left, right in ((upper, real, imag), (lower, -imag, real)):
                for columns, value in ((slice(0, 128), left), (slice(128, 256), right)):
                    high = value.astype(jnp.bfloat16)
                    lane_u[0, rows, columns] = high
                    lane_u[1, rows, columns] = (value - high.astype(jnp.float32)).astype(jnp.bfloat16)
            lane_a[upper, :128] = near
            lane_a[upper, 128:] = jnp.zeros_like(near)
            lane_a[lower, :128] = jnp.zeros_like(near)
            lane_a[lower, 128:] = near
            return carry

        lax.fori_loop(0, 8, body, 0)

    def build_trig():
        gamma = gamma_ref[0]

        def body(i, carry):
            b, r = i // 32, i % 32
            sine, cosine = sincos(gamma * energy[b, r].astype(jnp.float32))
            trig[0, b, r] = cosine
            trig[1, b, r] = sine
            return carry

        lax.fori_loop(0, 128, body, 0)

    def tile_bits_derivative():
        def body(i, acc):
            b, r = i // 32, i % 32
            near_re, near_im = zero, zero
            for bit in range(5):
                far = r + (1 << bit) - (2 << bit) * ((r // (1 << bit)) % 2)
                near_re = near_re + local_in[b, 0, far]
                near_im = near_im + local_in[b, 1, far]
            return acc + inner((local_in[b, 2, r], local_in[b, 3, r]), (near_re, near_im))

        total[1] += lax.fori_loop(0, 128, body, zero) * consts[8]

    build_lanes()
    build_trig()
    tile_bits_derivative()
    for j in range(STEPS):
        for p in range(3):
            wait_there(0, p, j)
            mix_axis(0, p, j)
            start_back(0, p, j)

    def core_copy(f, p, j):
        chunk, rows = STEPS * p + j, pl.ds(*PARTS[p][j])
        return home.at[f, :, :, rows], other.at[:, :, rows], c_send.at[chunk], c_recv.at[chunk], core_peer

    for f in range(2):
        for j in range(STEPS):
            with_core = [p for p in range(3) if core_first(p, j) == (f == 0)]
            for p in range(3):
                wait_back(f, p, j)
                if p in with_core:
                    send(*core_copy(f, p, j))
            for p in range(3):
                if p not in with_core:
                    mix_lanes(f, p, j)
                    start_there(f + 1, p, j)
            for p in with_core:
                wait_bytes(other.at[:, :, pl.ds(*PARTS[p][j])], c_recv.at[STEPS * p + j])
                mix_core_and_blocks(f, p, j)
                start_there(f + 1, p, j)
        if f == 0:
            for j in range(STEPS):
                for p in range(3):
                    wait_there(1, p, j)
                    mix_axis(1, p, j)
                    start_back(1, p, j)
    for p in range(3):
        wait_energy(p)
    for j in range(STEPS):
        for p in range(3):
            wait_there(2, p, j)
            mix_axis(2, p, j)
            if j < EARLY:
                start_back(2, p, j)

    stages = ((group[1:], 0), (plane[1:], 7))
    results = (o0, o1, o2, o3)

    def start_sum(stage):
        targets, first = stages[stage]
        for k, device in enumerate(targets):
            send(relay.at[stage, :2], landed.at[first + k, :2], red_send.at[stage], red_recv.at[stage], device)

    def finish_sum(stage):
        targets, first = stages[stage]
        count = len(targets)
        wait_bytes(landed.at[pl.ds(first, count), :2], red_recv.at[stage])
        terms = [relay[stage, :2]] + [landed[first + k, :2] for k in range(count)]
        while len(terms) > 1:
            terms = [terms[i] + terms[i + 1] for i in range(0, len(terms), 2)]
        relay[stage + 1, :2] = terms[0]

    def turn_back(p, j):
        r0, n = PARTS[p][j]

        def body(r, carry):
            for b in range(4):
                cosine, sine = trig[0, b, r], trig[1, b, r]
                for v in range(2):
                    re, im = home[2, b, 2 * v, r], home[2, b, 2 * v + 1, r]
                    results[2 * v][b, r] = re * cosine - im * sine
                    results[2 * v + 1][b, r] = re * sine + im * cosine
            return carry

        lax.fori_loop(r0, r0 + n, body, 0)

    for i in range(2):
        relay[0, i : i + 1] = jnp.sum(total[i], axis=0, keepdims=True)
    start_sum(0)
    for j in range(EARLY, STEPS):
        for p in range(3):
            start_back(2, p, j)
    for j in range(STEPS):
        for p in range(3):
            rows = pl.ds(*PARTS[p][j])
            wait_sent(0, p, j)
            wait_sent(1, p, j)
            wait_bytes(other.at[:, :, rows], c_send.at[STEPS * p + j])
    for j in range(STEPS):
        for p in range(3):
            wait_back(2, p, j)
            turn_back(p, j)
        if j == 0:
            finish_sum(0)
            start_sum(1)
    for j in range(STEPS):
        for p in range(3):
            wait_sent(2, p, j)
    finish_sum(1)
    scale = jnp.float32(1.0 / 16777216.0)
    gamma_out[0] = jnp.sum(relay[2, 0:1]) * scale
    beta_out[0] = jnp.sum(relay[2, 1:2]) * scale
    for stage, count in ((0, 7), (1, 15)):
        wait_bytes(landed.at[pl.ds(0, count), :2], red_send.at[stage])


def store_kernel(i0, i1, i2, i3, o0, o1, o2, o3, sem):
    copies = []
    for k, (source, target) in enumerate(((i0, o0), (i1, o1), (i2, o2), (i3, o3))):
        for b in range(STORES):
            rows = pl.ds(b * (4 // STORES), 4 // STORES)
            copies.append(pltpu.make_async_copy(source.at[rows], target.at[rows], sem.at[k, b]))
    for copy in copies:
        copy.start()
    for copy in copies:
        copy.wait()


def per_device(state_real, state_imag, adjoint_real, adjoint_imag, energies, gamma_angle, beta_angle):
    shape = (4, 32, 8, 128)
    args = [v.reshape(shape) for v in (state_real, state_imag, adjoint_real, adjoint_imag, energies)]
    hbm = pl.BlockSpec(memory_space=pltpu.HBM)
    vmem = pl.BlockSpec(memory_space=pltpu.VMEM)
    smem = pl.BlockSpec(memory_space=pltpu.SMEM)
    f32 = jnp.float32
    dma = pltpu.SemaphoreType.DMA
    big = pltpu.VMEM(shape, f32)
    one = jax.ShapeDtypeStruct((1,), f32)
    results = pl.pallas_call(
        kernel,
        out_shape=(big, big, big, big, one, one),
        in_specs=[smem, smem] + [hbm] * 5,
        out_specs=(vmem, vmem, vmem, vmem, smem, smem),
        scratch_shapes=[
            pltpu.VMEM((3, 3, 4, 32, 8, 128), f32),
            pltpu.VMEM((3, 4, 4, 32, 8, 128), f32),
            pltpu.VMEM((4, 4, 32, 8, 128), f32),
            pltpu.VMEM((4, 4, 32, 8, 128), f32),
            pltpu.VMEM((4, 4, 32, 8, 128), f32),
            pltpu.VMEM(shape, jnp.int32),
            pltpu.VMEM((3, 32, 8, 128), jnp.int32),
            pltpu.VMEM((2,) + shape, f32),
            pltpu.VMEM((9, 8, 128), f32),
            pltpu.VMEM((2, 256, 256), jnp.bfloat16),
            pltpu.VMEM((256, 256), jnp.bfloat16),
            pltpu.VMEM((2, 8, 128), f32),
            pltpu.VMEM((3, 8, 128), f32),
            pltpu.VMEM((22, 8, 128), f32),
            dma((3, 3 * STEPS)),
            dma((3, 3 * STEPS)),
            dma((3, 3 * STEPS)),
            dma((3, 3 * STEPS)),
            dma((3 * STEPS,)),
            dma((3 * STEPS,)),
            dma((3,)),
            dma((3,)),
            dma((5,)),
            dma((2,)),
            dma((2,)),
        ],
        compiler_params=pltpu.CompilerParams(
            collective_id=0, has_side_effects=True, vmem_limit_bytes=58 << 20
        ),
        cost_estimate=pl.CostEstimate(flops=2 << 30, bytes_accessed=5 << 20, transcendentals=0),
    )(gamma_angle, beta_angle, *args)
    moved = pl.pallas_call(
        store_kernel,
        out_shape=(jax.ShapeDtypeStruct(shape, f32),) * 4,
        in_specs=[vmem] * 4,
        out_specs=(pl.BlockSpec(memory_space=pltpu.HBM),) * 4,
        scratch_shapes=[dma((4, STORES))],
    )(*(pltpu.with_memory_space_constraint(v, pltpu.VMEM) for v in results[:4]))
    return tuple(v.reshape(-1) for v in moved) + (results[4], results[5])


def solution(mesh):
    whole = P(AXES)
    return jax.shard_map(
        per_device,
        mesh=mesh,
        in_specs=(whole,) * 5 + (P(), P()),
        out_specs=(whole,) * 4 + (P(), P()),
        check_vma=False,
    )
```

```python
import functools
import math

import jax
import jax.numpy as jnp
from jax import lax
from jax.experimental import pallas as pl
from jax.experimental.pallas import tpu as pltpu
from jax.sharding import PartitionSpec as P


MESH = pl.DeviceIdType.MESH
AXES = ("gx", "gy", "gz")
STEPS = 4
EARLY = 2


def core_first(p, j):
    return j % 2 == 1


STORES = 4


def cut(first, count):
    sizes = [count // STEPS + (STEPS - 1 - i < count % STEPS) for i in range(STEPS)]
    return tuple((first + sum(sizes[:i]), sizes[i]) for i in range(STEPS))


PARTS = (cut(0, 11), cut(11, 11), cut(22, 10))


def sincos(angle):
    turns = jnp.floor(angle * jnp.float32(2.0 / math.pi) + 0.5)
    rest = angle - turns * jnp.float32(1.5703125)
    rest = rest - turns * jnp.float32(4.837512969970703125e-4)
    rest = rest - turns * jnp.float32(7.54978995489188216e-8)
    square = rest * rest
    sine = ((-1.9515295891e-4 * square + 8.3321608736e-3) * square - 1.6666654611e-1) * square * rest + rest
    cosine = (
        ((2.443315711809948e-5 * square - 1.388731625493765e-3) * square + 4.166664568298827e-2) * square * square
        - 0.5 * square
        + 1.0
    )
    quadrant = turns - 4.0 * jnp.floor(turns * 0.25)
    odd = (quadrant == 1.0) | (quadrant == 3.0)
    sine_out = jnp.where(odd, cosine, sine)
    cosine_out = jnp.where(odd, sine, cosine)
    sine_out = jnp.where(quadrant >= 2.0, -sine_out, sine_out)
    cosine_out = jnp.where((quadrant == 1.0) | (quadrant == 2.0), -cosine_out, cosine_out)
    return sine_out, cosine_out


def inner(a, s):
    return a[0] * s[1] - a[1] * s[0]


def add(u, v):
    return u[0] + v[0], u[1] + v[1]


def turn(c, s, own, other):
    return c * own[0] - s * other[1], c * own[1] + s * other[0]


def mix_four(cc, ss, sc, x):
    outer, middle = add(x[0], x[3]), add(x[1], x[2])
    outer_re, outer_im = sc * outer[0], sc * outer[1]
    middle_re, middle_im = sc * middle[0], sc * middle[1]
    y = []
    for own, far, near_re, near_im in (
        (x[0], x[3], middle_re, middle_im),
        (x[1], x[2], outer_re, outer_im),
        (x[2], x[1], outer_re, outer_im),
        (x[3], x[0], middle_re, middle_im),
    ):
        y.append((cc * own[0] - ss * far[0] - near_im, cc * own[1] - ss * far[1] + near_re))
    return y, outer, middle


def kernel(
    gamma_ref, beta_ref, sr, si, ar, ai, energy_hbm,
    o0, o1, o2, o3, gamma_out, beta_out,
    mid, home, other, home_b, local_in, energy, energy_mid, trig, consts, lane_u, lane_a, total, relay, landed,
    t_send, t_recv, r_send, r_recv, c_send, c_recv, e_send, e_recv, in_sem, red_send, red_recv,
):
    gx, gy, gz = (lax.axis_index(name) for name in AXES)
    x_lo, z, core = gz // 8, (gz // 2) % 4, gz % 2
    flip_core = gz + 1 - 2 * core

    def flips(v):
        return v, v + 1 - 2 * (v % 2), v + 2 - 4 * (v // 2), 3 - v

    place = (2 * gx + x_lo, gy, z)
    blocks = tuple(flips(v) for v in place)
    x_flip = gz + 8 - 16 * x_lo
    peers = (
        (None, (gx, gy, x_flip), (1 - gx, gy, gz), (1 - gx, gy, x_flip)),
        (None,) + tuple((gx, blocks[1][k], gz) for k in (1, 2, 3)),
        (None,) + tuple((gx, gy, gz + 2 * (blocks[2][k] - z)) for k in (1, 2, 3)),
    )
    core_peer = (gx, gy, flip_core)
    group = []
    for k in range(4):
        base = gz + 2 * (blocks[2][k] - z)
        group += [(gx, gy, base), (gx, gy, base + 1 - 2 * core)]

    plane = []
    for i in range(4):
        over, along = ((gx, gz), (gx, x_flip), (1 - gx, gz), (1 - gx, x_flip))[i]
        plane += [(over, blocks[1][k], along) for k in range(4)]

    ins = (sr, si, ar, ai)

    loads = []
    for i, ref in enumerate(ins):
        loads.append(pltpu.make_async_copy(ref, local_in.at[:, i], in_sem.at[i]))
    loads.append(pltpu.make_async_copy(energy_hbm, energy, in_sem.at[4]))

    barrier = pltpu.get_barrier_semaphore()
    greeted = [core_peer] + [peers[axis][k] for axis in range(3) for k in (1, 2, 3)]
    for load in loads[:4]:
        load.start()
    for device in greeted:
        pl.semaphore_signal(barrier, inc=1, device_id=device, device_id_type=MESH)

    def send(src, dst, send_sem, recv_sem, device):
        pltpu.make_async_remote_copy(
            src_ref=src, dst_ref=dst, send_sem=send_sem, recv_sem=recv_sem, device_id=device, device_id_type=MESH
        ).start()

    def wait_bytes(ref, sem):
        pltpu.make_async_copy(ref, ref, sem).wait()

    def source_of(f, p, j):
        if f == 0:
            return local_in
        return home_b if core_first(p, j) == (f == 1) else home.at[f - 1]

    def start_there(f, p, j, arrays=slice(None)):
        axis = (p + f) % 3
        r0, n = PARTS[p][j]
        rows = pl.ds(r0, n)
        ss, rs = t_send.at[f, STEPS * p + j], t_recv.at[f, STEPS * p + j]
        source = source_of(f, p, j)
        for k in (3, 1, 2):
            send(source.at[blocks[axis][k], arrays, rows], mid.at[f, k - 1, arrays, rows], ss, rs, peers[axis][k])

    def part_rows(p):
        return pl.ds(PARTS[p][0][0], sum(n for _, n in PARTS[p]))

    def start_energy(p):
        axis, rows = (p + 2) % 3, part_rows(p)
        for k in (3, 1, 2):
            block = blocks[axis][k]
            send(energy_hbm.at[block, rows], energy_mid.at[k - 1, rows], e_send.at[p], e_recv.at[p], peers[axis][k])

    def wait_energy(p):
        wait_bytes(energy_mid.at[:, part_rows(p)], e_recv.at[p])
        wait_bytes(energy_mid.at[:, part_rows(p)], e_send.at[p])

    def start_back(f, p, j):
        axis = (p + f) % 3
        r0, n = PARTS[p][j]
        me, rows = place[axis], pl.ds(r0, n)
        ss, rs = r_send.at[f, STEPS * p + j], r_recv.at[f, STEPS * p + j]
        for k in (3, 1, 2):
            send(mid.at[f, k - 1, :, rows], home.at[f, me, :, rows], ss, rs, peers[axis][k])

    def wait_there(f, p, j):
        rows = pl.ds(*PARTS[p][j])
        wait_bytes(mid.at[f, :, :, rows], t_recv.at[f, STEPS * p + j])

    def wait_back(f, p, j):
        rows = pl.ds(*PARTS[p][j])
        wait_bytes(mid.at[f, :, :, rows], r_recv.at[f, STEPS * p + j])

    def wait_sent(f, p, j):
        rows = pl.ds(*PARTS[p][j])
        wait_bytes(mid.at[f, :, :, rows], t_send.at[f, STEPS * p + j])
        wait_bytes(mid.at[f, :, :, rows], r_send.at[f, STEPS * p + j])

    zero = jnp.zeros((8, 128), jnp.float32)

    sub = lax.broadcasted_iota(jnp.int32, (8, 128), 0)

    def far_row(x, bit):
        step = 1 << bit
        if bit == 2:
            return pltpu.roll(x, 4, 0)
        return jnp.where((sub >> bit) & 1 == 1, pltpu.roll(x, step, 0), pltpu.roll(x, 8 - step, 0))

    def mix_axis(f, p, j):
        r0, n = PARTS[p][j]
        me, source = place[(p + f) % 3], source_of(f, p, j)
        cc, ss, sc = (consts[i + (5 if f == 0 else 0)] for i in range(3))
        c, sn = consts[3], consts[4]

        def body(r, accs):
            acc, acc_gamma = accs
            x = []
            for v in range(2):
                own = source[me, 2 * v, r], source[me, 2 * v + 1, r]
                x.append([own] + [(mid[f, k, 2 * v, r], mid[f, k, 2 * v + 1, r]) for k in range(3)])
            s, s_outer, s_middle = mix_four(cc, ss, sc, x[0])
            a, a_outer, a_middle = mix_four(cc, ss, sc, x[1])
            acc = acc + inner(a_outer, s_middle) + inner(a_middle, s_outer)
            for b in range(4):
                if f == 1:
                    for bit in range(3):
                        s_far = far_row(s[b][0], bit), far_row(s[b][1], bit)
                        a_far = far_row(a[b][0], bit), far_row(a[b][1], bit)
                        acc = acc + inner(a[b], s_far)
                        s[b] = turn(c, sn, s[b], s_far)
                        a[b] = turn(c, sn, a[b], a_far)
                if f == 2:
                    level = energy_mid[b - 1, r] if b else energy[me, r]
                    acc_gamma = acc_gamma + level.astype(jnp.float32) * inner(a[b], s[b])
                for i, value in enumerate((*s[b], *a[b])):
                    if b:
                        mid[f, b - 1, i, r] = value
                    else:
                        home[f, me, i, r] = value
            return acc, acc_gamma

        acc, acc_gamma = lax.fori_loop(r0, r0 + n, body, (zero, zero))
        total[1] += acc * consts[8] if f == 0 else acc
        if f == 2:
            total[0] += acc_gamma

    def mix_core_and_blocks(f, p, j):
        r0, n = PARTS[p][j]
        cc, ss, sc, c, sn = (consts[i] for i in range(5))

        def body(r, acc):
            x = []
            for v in range(2):
                x.append([])
                for b in range(4):
                    own = home[f, b, 2 * v, r], home[f, b, 2 * v + 1, r]
                    far = other[b, 2 * v, r], other[b, 2 * v + 1, r]
                    if v == 0:
                        x[v].append((own, far))
                    else:
                        acc = acc + inner(own, x[0][b][1])
                        x[v].append((own, far))
            x = [[turn(c, sn, own, far) for own, far in half] for half in x]
            s, s_outer, s_middle = mix_four(cc, ss, sc, x[0])
            a, a_outer, a_middle = mix_four(cc, ss, sc, x[1])
            for v, y in ((0, s), (1, a)):
                for b in range(4):
                    home_b[b, 2 * v, r] = y[b][0]
                    home_b[b, 2 * v + 1, r] = y[b][1]
            return acc + inner(a_outer, s_middle) + inner(a_middle, s_outer)

        total[1] += lax.fori_loop(r0, r0 + n, body, zero)

    def mix_lanes(f, p, j):
        r0, n = PARTS[p][j]
        rows, size = pl.ds(r0, n), n * 8

        def halves(v):
            parts = []
            for b in range(4):
                re = home[f, b, 2 * v, rows].reshape(size, 128)
                im = home[f, b, 2 * v + 1, rows].reshape(size, 128)
                parts.append(jnp.concatenate([re, im], axis=1))
            full = jnp.concatenate(parts, axis=0)
            high = full.astype(jnp.bfloat16)
            return full, high, (full - high.astype(jnp.float32)).astype(jnp.bfloat16)

        dot = functools.partial(jnp.dot, preferred_element_type=jnp.float32)
        u_high, u_low, near = lane_u[0], lane_u[1], lane_a[...]
        _, s_high, s_low = halves(0)
        full, a_high, a_low = halves(1)
        s_near = dot(s_high, near) + dot(s_low, near)
        part = inner((full[:, :128], full[:, 128:]), (s_near[:, :128], s_near[:, 128:]))
        total[1] += jnp.sum(part.reshape(4 * n, 8, 128), axis=0)
        for v, (high, low) in enumerate(((s_high, s_low), (a_high, a_low))):
            mixed = dot(high, u_high) + (dot(low, u_high) + dot(high, u_low))
            for b in range(4):
                home[f, b, 2 * v, rows] = mixed[b * size : (b + 1) * size, :128].reshape(n, 8, 128)
                home[f, b, 2 * v + 1, rows] = mixed[b * size : (b + 1) * size, 128:].reshape(n, 8, 128)

    sn, c = sincos(jnp.full((8, 128), beta_ref[0], jnp.float32))
    scale_tiles = c * c * c * c * c
    tangent = sn / c
    for i, value in enumerate((c * c, sn * sn, sn * c, c, sn)):
        consts[i] = value
    for i in range(3):
        consts[5 + i] = consts[i] * scale_tiles
    consts[8] = scale_tiles * scale_tiles
    total[0] = zero
    total[1] = zero

    def tile_pair(u, v):
        return (
            (u[0] - tangent * v[1], u[1] + tangent * v[0]),
            (v[0] - tangent * u[1], v[1] + tangent * u[0]),
        )

    def mix_tiles(b, v, places, bits):
        x = [(local_in[b, 2 * v, r], local_in[b, 2 * v + 1, r]) for r in places]
        for bit in range(bits):
            for k in range(1 << bits):
                if not k >> bit & 1:
                    x[k], x[k + (1 << bit)] = tile_pair(x[k], x[k + (1 << bit)])
        for r, (re, im) in zip(places, x):
            local_in[b, 2 * v, r] = re
            local_in[b, 2 * v + 1, r] = im

    def low_bits(v, i, carry):
        mix_tiles(i // 4, v, [8 * (i % 4) + k for k in range(8)], 3)
        return carry

    def high_bits(v, i, carry):
        for half in range(2):
            mix_tiles(i // 4, v, [2 * (i % 4) + half + 8 * k for k in range(4)], 2)
        return carry

    pl.semaphore_wait(barrier, len(greeted))
    for p in range(3):
        start_energy(p)
    for v in range(2):
        for load in loads[2 * v : 2 * v + 2]:
            load.wait()
        lax.fori_loop(0, 16, functools.partial(low_bits, v), 0)
        lax.fori_loop(0, 16, functools.partial(high_bits, v), 0)
        for p in range(3):
            start_there(0, p, 0, pl.ds(2 * v, 2))
    for j in range(1, STEPS):
        for p in range(3):
            start_there(0, p, j)
    loads[4].start()

    def build_lanes():
        c_row, s_row = (jnp.concatenate([consts[i], consts[i]], axis=0) for i in (3, 4))

        def body(i, carry):
            row = lax.broadcasted_iota(jnp.int32, (16, 128), 0) + 16 * i
            bits = row ^ lax.broadcasted_iota(jnp.int32, (16, 128), 1)
            size = jnp.ones((16, 128), jnp.float32)
            ones = jnp.zeros((16, 128), jnp.int32)
            for bit in range(7):
                on = (bits >> bit) & 1
                size = size * jnp.where(on == 1, s_row, c_row)
                ones = ones + on
            real = jnp.where(ones % 4 == 0, size, jnp.where(ones % 4 == 2, -size, 0.0))
            imag = jnp.where(ones % 4 == 1, size, jnp.where(ones % 4 == 3, -size, 0.0))
            near = jnp.where(ones == 1, 1.0, 0.0).astype(jnp.bfloat16)
            upper = pl.ds(pl.multiple_of(16 * i, 16), 16)
            lower = pl.ds(pl.multiple_of(128 + 16 * i, 16), 16)
            for rows, left, right in ((upper, real, imag), (lower, -imag, real)):
                for columns, value in ((slice(0, 128), left), (slice(128, 256), right)):
                    high = value.astype(jnp.bfloat16)
                    lane_u[0, rows, columns] = high
                    lane_u[1, rows, columns] = (value - high.astype(jnp.float32)).astype(jnp.bfloat16)
            lane_a[upper, :128] = near
            lane_a[upper, 128:] = jnp.zeros_like(near)
            lane_a[lower, :128] = jnp.zeros_like(near)
            lane_a[lower, 128:] = near
            return carry

        lax.fori_loop(0, 8, body, 0)

    def build_trig():
        gamma = gamma_ref[0]

        def body(i, carry):
            b, r = i // 32, i % 32
            sine, cosine = sincos(gamma * energy[b, r].astype(jnp.float32))
            trig[0, b, r] = cosine
            trig[1, b, r] = sine
            return carry

        lax.fori_loop(0, 128, body, 0)

    def tile_bits_derivative():
        def body(i, acc):
            b, r = i // 32, i % 32
            near_re, near_im = zero, zero
            for bit in range(5):
                far = r + (1 << bit) - (2 << bit) * ((r // (1 << bit)) % 2)
                near_re = near_re + local_in[b, 0, far]
                near_im = near_im + local_in[b, 1, far]
            return acc + inner((local_in[b, 2, r], local_in[b, 3, r]), (near_re, near_im))

        total[1] += lax.fori_loop(0, 128, body, zero) * consts[8]

    build_lanes()
    loads[4].wait()
    build_trig()
    tile_bits_derivative()
    for j in range(STEPS):
        for p in range(3):
            wait_there(0, p, j)
            mix_axis(0, p, j)
            start_back(0, p, j)

    def core_copy(f, p, j):
        chunk, rows = STEPS * p + j, pl.ds(*PARTS[p][j])
        return home.at[f, :, :, rows], other.at[:, :, rows], c_send.at[chunk], c_recv.at[chunk], core_peer

    for f in range(2):
        for j in range(STEPS):
            with_core = [p for p in range(3) if core_first(p, j) == (f == 0)]
            for p in range(3):
                wait_back(f, p, j)
                if p in with_core:
                    send(*core_copy(f, p, j))
            for p in range(3):
                if p not in with_core:
                    mix_lanes(f, p, j)
                    start_there(f + 1, p, j)
            for p in with_core:
                wait_bytes(other.at[:, :, pl.ds(*PARTS[p][j])], c_recv.at[STEPS * p + j])
                mix_core_and_blocks(f, p, j)
                start_there(f + 1, p, j)
        if f == 0:
            for j in range(STEPS):
                for p in range(3):
                    wait_there(1, p, j)
                    mix_axis(1, p, j)
                    start_back(1, p, j)
    for p in range(3):
        wait_energy(p)
    for j in range(STEPS):
        for p in range(3):
            wait_there(2, p, j)
            mix_axis(2, p, j)
            if j < EARLY:
                start_back(2, p, j)

    stages = ((group[1:], 0), (plane[1:], 7))
    results = (o0, o1, o2, o3)

    def start_sum(stage):
        targets, first = stages[stage]
        for k, device in enumerate(targets):
            send(relay.at[stage, :2], landed.at[first + k, :2], red_send.at[stage], red_recv.at[stage], device)

    def finish_sum(stage):
        targets, first = stages[stage]
        count = len(targets)
        wait_bytes(landed.at[pl.ds(first, count), :2], red_recv.at[stage])
        terms = [relay[stage, :2]] + [landed[first + k, :2] for k in range(count)]
        while len(terms) > 1:
            terms = [terms[i] + terms[i + 1] for i in range(0, len(terms), 2)]
        relay[stage + 1, :2] = terms[0]

    def turn_back(p, j):
        r0, n = PARTS[p][j]

        def body(r, carry):
            for b in range(4):
                cosine, sine = trig[0, b, r], trig[1, b, r]
                for v in range(2):
                    re, im = home[2, b, 2 * v, r], home[2, b, 2 * v + 1, r]
                    results[2 * v][b, r] = re * cosine - im * sine
                    results[2 * v + 1][b, r] = re * sine + im * cosine
            return carry

        lax.fori_loop(r0, r0 + n, body, 0)

    for i in range(2):
        relay[0, i : i + 1] = jnp.sum(total[i], axis=0, keepdims=True)
    start_sum(0)
    for j in range(EARLY, STEPS):
        for p in range(3):
            start_back(2, p, j)
    for j in range(STEPS):
        for p in range(3):
            rows = pl.ds(*PARTS[p][j])
            wait_sent(0, p, j)
            wait_sent(1, p, j)
            wait_bytes(other.at[:, :, rows], c_send.at[STEPS * p + j])
    for j in range(STEPS):
        for p in range(3):
            wait_back(2, p, j)
            turn_back(p, j)
        if j == 0:
            finish_sum(0)
            start_sum(1)
    for j in range(STEPS):
        for p in range(3):
            wait_sent(2, p, j)
    finish_sum(1)
    scale = jnp.float32(1.0 / 16777216.0)
    gamma_out[0] = jnp.sum(relay[2, 0:1]) * scale
    beta_out[0] = jnp.sum(relay[2, 1:2]) * scale
    for stage, count in ((0, 7), (1, 15)):
        wait_bytes(landed.at[pl.ds(0, count), :2], red_send.at[stage])


def store_kernel(i0, i1, i2, i3, o0, o1, o2, o3, sem):
    copies = []
    for k, (source, target) in enumerate(((i0, o0), (i1, o1), (i2, o2), (i3, o3))):
        for b in range(STORES):
            rows = pl.ds(b * (4 // STORES), 4 // STORES)
            copies.append(pltpu.make_async_copy(source.at[rows], target.at[rows], sem.at[k, b]))
    for copy in copies:
        copy.start()
    for copy in copies:
        copy.wait()


def per_device(state_real, state_imag, adjoint_real, adjoint_imag, energies, gamma_angle, beta_angle):
    shape = (4, 32, 8, 128)
    args = [v.reshape(shape) for v in (state_real, state_imag, adjoint_real, adjoint_imag, energies)]
    hbm = pl.BlockSpec(memory_space=pltpu.HBM)
    vmem = pl.BlockSpec(memory_space=pltpu.VMEM)
    smem = pl.BlockSpec(memory_space=pltpu.SMEM)
    f32 = jnp.float32
    dma = pltpu.SemaphoreType.DMA
    big = pltpu.VMEM(shape, f32)
    one = jax.ShapeDtypeStruct((1,), f32)
    results = pl.pallas_call(
        kernel,
        out_shape=(big, big, big, big, one, one),
        in_specs=[smem, smem] + [hbm] * 5,
        out_specs=(vmem, vmem, vmem, vmem, smem, smem),
        scratch_shapes=[
            pltpu.VMEM((3, 3, 4, 32, 8, 128), f32),
            pltpu.VMEM((3, 4, 4, 32, 8, 128), f32),
            pltpu.VMEM((4, 4, 32, 8, 128), f32),
            pltpu.VMEM((4, 4, 32, 8, 128), f32),
            pltpu.VMEM((4, 4, 32, 8, 128), f32),
            pltpu.VMEM(shape, jnp.int32),
            pltpu.VMEM((3, 32, 8, 128), jnp.int32),
            pltpu.VMEM((2,) + shape, f32),
            pltpu.VMEM((9, 8, 128), f32),
            pltpu.VMEM((2, 256, 256), jnp.bfloat16),
            pltpu.VMEM((256, 256), jnp.bfloat16),
            pltpu.VMEM((2, 8, 128), f32),
            pltpu.VMEM((3, 8, 128), f32),
            pltpu.VMEM((22, 8, 128), f32),
            dma((3, 3 * STEPS)),
            dma((3, 3 * STEPS)),
            dma((3, 3 * STEPS)),
            dma((3, 3 * STEPS)),
            dma((3 * STEPS,)),
            dma((3 * STEPS,)),
            dma((3,)),
            dma((3,)),
            dma((5,)),
            dma((2,)),
            dma((2,)),
        ],
        compiler_params=pltpu.CompilerParams(
            collective_id=0, has_side_effects=True, vmem_limit_bytes=58 << 20
        ),
        cost_estimate=pl.CostEstimate(flops=2 << 30, bytes_accessed=5 << 20, transcendentals=0),
    )(gamma_angle, beta_angle, *args)
    moved = pl.pallas_call(
        store_kernel,
        out_shape=(jax.ShapeDtypeStruct(shape, f32),) * 4,
        in_specs=[vmem] * 4,
        out_specs=(pl.BlockSpec(memory_space=pltpu.HBM),) * 4,
        scratch_shapes=[dma((4, STORES))],
    )(*(pltpu.with_memory_space_constraint(v, pltpu.VMEM) for v in results[:4]))
    return tuple(v.reshape(-1) for v in moved) + (results[4], results[5])


def solution(mesh):
    whole = P(AXES)
    return jax.shard_map(
        per_device,
        mesh=mesh,
        in_specs=(whole,) * 5 + (P(), P()),
        out_specs=(whole,) * 4 + (P(), P()),
        check_vma=False,
    )
```
